512 devices in a mesh: tm: 32 (over z_lo, y), mp: 16 (over x, z_hi, core).
Axes of the slice: x: 4, y: 4, z: 16 (z_hi: 2, z_lo: 8; z = z_hi * 8 + z_lo), core: 2. Of those that a mesh axis runs over, the one named last changes fastest.
Arguments:
- queries: bfloat16 [6144, 4096], P('tm', 'mp'), may hold values from -8 to 8
- d_queries: bfloat16 [6144, 4096], P('tm', 'mp'), may hold values from -6 to 6
- key_rows: bfloat16 [6144, 4096], P('tm', 'mp'), may hold values from -8 to 8
- value_rows: bfloat16 [6144, 4096], P('tm', 'mp'), may hold values from -6 to 6
- d_key_rows: bfloat16 [6144, 4096], P('tm', 'mp'), may hold values from -6 to 6
- d_value_rows: bfloat16 [6144, 4096], P('tm', 'mp'), may hold values from -6 to 6
- live_flags: int32 [6144], P('tm'), may hold values from 0 to 1, as said below
- out_weight: bfloat16 [4096, 5120], P('mp'), may hold values from -1 to 1
- gate_scale: float32 [5120], P('mp'), may hold values from 0.25 to 1.75
- tokens: bfloat16 [6144, 5120], P('tm', 'mp'), may hold values from -6 to 6
- d_tokens: bfloat16 [6144, 5120], P('tm', 'mp'), may hold values from -6 to 6
Outputs:
- result: bfloat16 [6144, 5120], P('tm', 'mp')
- d_result: bfloat16 [6144, 5120], P('tm', 'mp')
The draws below stay inside these ranges and needn't reach their ends.
Inputs may be any that keep to these rules, and one draw needn't show every extreme that they name: live_flags are equal within each aligned run of 32 tokens.
All inputs are finite; a program needn't handle non-finite values.
Results may differ from the reference program's by a relative error of at most 0.019.
Values may be sent and summed in bfloat16 or wider, within the bound.
No kernel may reach another device: no remote copies, remote signals or barrier semaphores. Data moves between devices by JAX's collectives and lax.ppermute only.
A program may use at most 128 MiB of HBM per device.

```python
import math
import jax
import jax.numpy as jnp
from jax import lax

D = 5120
HD = 128
H_DEV = 2
FRAME = 32
HEADS = 32
TOKENS = 6144
N_MP = 16


def drawn_field(key):
    values = 1.2 * jax.random.normal(key, (TOKENS, HEADS * HD), jnp.float32)
    return values


def draw_queries(key, part):
    values = drawn_field(jax.random.fold_in(key, 11))
    return jnp.clip(values, -8.0, 8.0).astype(jnp.bfloat16)


def draw_key_rows(key, part):
    values = drawn_field(jax.random.fold_in(key, 13))
    return jnp.clip(values, -8.0, 8.0).astype(jnp.bfloat16)


def draw_live_flags(key, part):
    frames = jax.random.randint(jax.random.fold_in(key, 17), (TOKENS // FRAME,), 0, 4)
    flags = (frames > 0).astype(jnp.int32)
    return jnp.repeat(flags, FRAME)


def levels(rng, dims, cuts, least, top_value):
    def one(axis_at, shards_of):
        draws = jax.random.uniform(jax.random.fold_in(jax.random.fold_in(rng, 6), axis_at), (shards_of,), jnp.float32, least / len(cuts), top_value / len(cuts))
        return jnp.repeat(jnp.exp(draws), dims[axis_at] // shards_of).reshape((-1,) + (1,) * (len(dims) - axis_at - 1))

    loudness = one(*cuts[0])
    for cut in cuts[1:]:
        loudness = loudness * one(*cut)
    return loudness


def noise(own_key, extent, spread, most, cuts=(), dtype=jnp.bfloat16):
    drawn = jax.random.normal(own_key, extent, jnp.float32) * spread
    if len(cuts) > 0:
        drawn = levels(own_key, extent, cuts, -0.22, 0.18) * drawn
    return jnp.clip(drawn, min=-most, max=most).astype(dtype)


def setup_inputs(seed: int = 0) -> dict:
    seeds = jax.random.split(jax.random.key(seed), 12)
    return {
        "queries": draw_queries(jax.random.fold_in(seeds[11], 71), 0),
        "d_queries": noise(seeds[1], (TOKENS, HEADS * HD), 1.0, 6.0, ((0, 32), (1, 16))),
        "key_rows": draw_key_rows(jax.random.fold_in(seeds[11], 71), 0),
        "value_rows": noise(seeds[3], (TOKENS, HEADS * HD), 1.0, 6.0, ((0, 32), (1, 16))),
        "d_key_rows": noise(seeds[4], (TOKENS, HEADS * HD), 1.0, 6.0, ((0, 32), (1, 16))),
        "d_value_rows": noise(seeds[5], (TOKENS, HEADS * HD), 1.0, 6.0, ((0, 32), (1, 16))),
        "live_flags": draw_live_flags(jax.random.fold_in(seeds[11], 71), 0),
        "out_weight": noise(seeds[7], (HEADS * HD, D), (H_DEV * HD // 8) ** -0.5, 1.0, ((0, 16),)),
        "gate_scale": jnp.clip(1.0 + 0.15 * jax.random.normal(seeds[8], (D,), jnp.float32), 0.25, 1.75),
        "tokens": noise(seeds[9], (TOKENS, D), 1.0, 6.0, ((0, 32), (1, 16))),
        "d_tokens": noise(seeds[10], (TOKENS, D), 1.0, 6.0, ((0, 32), (1, 16))),
    }


def one_head(pieces):
    query_h, tangent_q, key_h, value_h, tangent_k, tangent_v = pieces
    factor = 1.0 / math.sqrt(HD)
    scores = jnp.dot(query_h, key_h.T, preferred_element_type=jnp.float32) * factor
    d_scores = (jnp.dot(tangent_q, key_h.T, preferred_element_type=jnp.float32) + jnp.dot(query_h, tangent_k.T, preferred_element_type=jnp.float32)) * factor
    peak = lax.optimization_barrier(jnp.max(scores, axis=1, keepdims=True))
    weights = jnp.exp(scores - peak)
    totals = lax.optimization_barrier(jnp.sum(weights, axis=1, keepdims=True))
    product = weights * d_scores
    slopes = lax.optimization_barrier(jnp.sum(product, axis=1, keepdims=True))
    weights_b = weights.astype(jnp.bfloat16)
    product_b = product.astype(jnp.bfloat16)
    primal = jnp.dot(weights_b, value_h, preferred_element_type=jnp.float32)
    tangent = jnp.dot(product_b, value_h, preferred_element_type=jnp.float32) + jnp.dot(weights_b, tangent_v, preferred_element_type=jnp.float32)
    outputs = primal / totals
    d_outputs = tangent / totals - slopes / totals * outputs
    return (outputs.astype(jnp.bfloat16), d_outputs.astype(jnp.bfloat16))

def reference(queries, d_queries, key_rows, value_rows, d_key_rows, d_value_rows, live_flags, out_weight, gate_scale, tokens, d_tokens):
    live_rows = live_flags[:, None] > 0

    def masked(matrix):
        return jnp.where(live_rows, matrix, jnp.zeros_like(matrix))

    def by_heads(matrix):
        return matrix.reshape(TOKENS, HEADS, HD).transpose(1, 0, 2)
    stacked = tuple((by_heads(matrix) for matrix in (queries, masked(d_queries), key_rows, value_rows, masked(d_key_rows), masked(d_value_rows))))
    outputs, d_outputs = lax.map(one_head, stacked)

    def regroup(heads_out):
        return heads_out.transpose(1, 0, 2).reshape(TOKENS, N_MP, H_DEV * HD).transpose(1, 0, 2)
    weight_groups = out_weight.reshape(N_MP, H_DEV * HD, D)

    def add_group(running, pieces):
        group_o, group_do, group_w = pieces
        part_y = jnp.dot(group_o, group_w, preferred_element_type=jnp.float32)
        part_dy = jnp.dot(group_do, group_w, preferred_element_type=jnp.float32)
        rounded = lax.optimization_barrier((part_y.astype(jnp.bfloat16), part_dy.astype(jnp.bfloat16)))
        return ((running[0] + rounded[0].astype(jnp.float32), running[1] + rounded[1].astype(jnp.float32)), None)
    blank_sum = jnp.zeros((TOKENS, D), jnp.float32)
    sums, unused = lax.scan(add_group, (blank_sum, blank_sum), (regroup(outputs), regroup(d_outputs), weight_groups))
    result = (tokens.astype(jnp.float32) + gate_scale * sums[0]).astype(jnp.bfloat16)
    d_result = (masked(d_tokens).astype(jnp.float32) + gate_scale * sums[1]).astype(jnp.bfloat16)
    return (result, d_result)
```

```python
import functools
import math

import jax
import jax.numpy as jnp
from jax import lax
from jax.experimental import pallas as pl
from jax.experimental.pallas import tpu as pltpu
from jax.sharding import PartitionSpec as P

HD = 128
FRAME = 32
NZ, NY, NX = 8, 4, 4
FACTOR = 1.0 / math.sqrt(HD)
LOG2E = math.log2(math.e)
STAT_ROWS = 16
BF = jnp.bfloat16
F32 = jnp.float32
VMEM_LIMIT = 44 * 1024 * 1024


def params():
    return pltpu.CompilerParams(vmem_limit_bytes=VMEM_LIMIT)


SMEM_SPEC = pl.BlockSpec(memory_space=pltpu.SMEM)
VMEM_SPEC = pl.BlockSpec(memory_space=pltpu.VMEM)
ANY_SPEC = pl.BlockSpec(memory_space=pl.ANY)


def over_z(k):
    return [(z * NY + y, (z ^ k) * NY + y) for z in range(NZ) for y in range(NY)]


def over_y(k):
    return [(z * NY + y, z * NY + (y + k) % NY) for z in range(NZ) for y in range(NY)]


def over_x(k):
    return [(x * 4 + r, (x + k) % NX * 4 + r) for x in range(NX) for r in range(4)]


def over_half():
    return [(i, i ^ 2) for i in range(4 * NX)]


def over_core():
    return [(i, i ^ 1) for i in range(4 * NX)]


def pack_kernel(odd, flags, q, dq, k, v, dk, dv, qd_own, qd_other, kv_own, kv_other):
    is_odd = odd[0] > 0
    for f in range(q.shape[0] // FRAME):
        rows = pl.ds(f * FRAME, FRAME)
        live = flags[f * FRAME] > 0

        def masked(ref):
            block = ref[rows, :]
            return jnp.where(live, block, jnp.zeros_like(block))

        blocks = (masked(dq), q[rows, :], k[rows, :], masked(dk), v[rows, :], masked(dv))
        for i, block in enumerate(blocks):
            first, second = block[:, :HD], block[:, HD:]
            own = jnp.where(is_odd, second, first)
            other = jnp.where(is_odd, first, second)
            if i < 2:
                at = slice(i * HD, (i + 1) * HD)
                qd_own[rows, at] = own
                qd_other[rows, at] = other
            else:
                at = slice((i - 2) * HD, (i - 1) * HD)
                kv_own[rows, at] = own
                kv_other[rows, at] = other


def in_three(value):
    high = value.astype(BF).astype(F32)
    middle = (value - high).astype(BF).astype(F32)
    low = (value - high - middle).astype(BF).astype(F32)
    return high, middle, low


def attend_kernel(pieces, *refs):
    kv_in, qd_in, outs = refs[:8], refs[8:16], refs[16:24]
    kv, qd, held, sems = refs[24:]
    rows = qd_in[0].shape[0]
    copies = []
    for i in range(8):
        at = pl.ds(i * rows, rows)
        copies.append(pltpu.make_async_copy(kv_in[i], kv.at[at], sems.at[i]))
        copies.append(pltpu.make_async_copy(qd_in[i], qd.at[at], sems.at[8 + i]))
    for copy in copies:
        copy.start()
    for copy in copies:
        copy.wait()
    count = rows * pieces
    contract = (((1,), (1,)), ((), ()))

    def step(j, carry):
        at = pl.ds(pl.multiple_of(j * count, count), count)
        both = qd[at, :]
        scores = lax.dot_general(both[:, HD:], kv[:, :HD], contract, preferred_element_type=F32)
        slopes = lax.dot_general(both, kv[:, : 2 * HD], contract, preferred_element_type=F32)
        scores = scores * (FACTOR * LOG2E)
        peak = jnp.max(scores, axis=1, keepdims=True)
        weights = jnp.exp2(scores - peak)
        total = jnp.sum(weights, axis=1, keepdims=True)
        product = weights * slopes
        slope = jnp.sum(product, axis=1, keepdims=True)
        weighted = jnp.dot(weights.astype(BF), kv[:, 2 * HD :], preferred_element_type=F32)
        tangent = jnp.dot(product.astype(BF), kv[:, 2 * HD : 3 * HD], preferred_element_type=F32)
        inverse = 1.0 / total
        mean = slope * (inverse * FACTOR)
        primal = weighted[:, :HD] * inverse
        tangent = (tangent * FACTOR + weighted[:, HD:]) * inverse - mean * primal
        lanes = lax.broadcasted_iota(jnp.int32, (count, HD), 1)
        stats = jnp.zeros((count, HD), F32)
        for i, part in enumerate(in_three(peak + jnp.log2(total)) + in_three(mean)):
            stats = jnp.where(lanes == i, part, stats)
        for p in range(pieces):
            mine = slice(p * rows, (p + 1) * rows)
            held[j * pieces + p, :rows, :HD] = primal[mine].astype(BF)
            held[j * pieces + p, :rows, HD:] = tangent[mine].astype(BF)
            tile = jnp.concatenate([stats[mine], jnp.zeros((2 * HD - rows, HD), F32)], axis=0)
            held[j * pieces + p, rows:, :] = tile.T[:STAT_ROWS].astype(BF)
        return carry

    lax.fori_loop(0, 8 // pieces, step, 0)
    back = [pltpu.make_async_copy(held.at[i], outs[i], sems.at[i]) for i in range(8)]
    for copy in back:
        copy.start()
    for copy in back:
        copy.wait()


def merge_kernel(place, *refs):
    parts, (keep, send) = refs[:8], refs[8:]
    rows = keep.shape[0]
    stats = jnp.concatenate([part[rows:, :] for part in parts], axis=0).astype(F32).T[:rows]

    def value(i, first):
        at = i * STAT_ROWS + first
        return stats[:, at : at + 1] + stats[:, at + 1 : at + 2] + stats[:, at + 2 : at + 3]

    merged = []
    for parity in range(2):
        group = range(parity, 8, 2)
        sizes = [value(i, 0) for i in group]
        means = [value(i, 3) for i in group]
        peak = functools.reduce(jnp.maximum, sizes)
        sizes = [jnp.exp2(size - peak) for size in sizes]
        inverse = 1.0 / sum(sizes)
        sizes = [size * inverse for size in sizes]
        mean = sum(size * m for size, m in zip(sizes, means))
        primal = jnp.zeros((rows, HD), F32)
        tangent = jnp.zeros((rows, HD), F32)
        for i, size, m in zip(group, sizes, means):
            a = parts[i][:rows, :HD].astype(F32)
            primal += size * a
            tangent += size * parts[i][:rows, HD:].astype(F32) + (size * (m - mean)) * a
        merged.append((primal.astype(BF), tangent.astype(BF)))
    odd = place[0] > 0
    core = place[1] > 0
    (own_p, own_t), (other_p, other_t) = merged
    for h, (p, t) in enumerate(
        (
            (jnp.where(odd, other_p, own_p), jnp.where(odd, other_t, own_t)),
            (jnp.where(odd, own_p, other_p), jnp.where(odd, own_t, other_t)),
        )
    ):
        at = slice(h * HD, (h + 1) * HD)
        keep[:, at] = jnp.where(core, t, p)
        send[:, at] = jnp.where(core, p, t)


def project_kernel(half, *refs):
    acts, w_own, w_other, (mine, theirs) = refs[:4], refs[4:8], refs[8:12], refs[12:]
    width = mine.shape[1]
    depth = w_own[0].shape[0]
    for second in range(2):
        at = slice(second * width, (second + 1) * width)
        total = jnp.zeros(mine.shape, F32)
        for i in range(4):
            total += jnp.dot(acts[i][:, :depth], w_own[i][:, at], preferred_element_type=F32)
            total += jnp.dot(acts[i][:, depth:], w_other[i][:, at], preferred_element_type=F32)

        @pl.when(half[0] == second)
        def _():
            mine[...] = total

        @pl.when(half[0] != second)
        def _():
            theirs[...] = total.astype(BF)


def add_kernel(core, mine, theirs, keep, send):
    total = (mine[...] + theirs[...].astype(F32)).astype(BF)
    width = keep.shape[1]
    first, second = total[:, :width], total[:, width:]
    is_second = core[0] > 0
    keep[...] = jnp.where(is_second, second, first)
    send[...] = jnp.where(is_second, first, second)


def finish_kernel(core, flags, keep, got, gate, tokens, d_tokens, result, d_result):
    is_second = core[0] > 0
    scale = gate[...]
    for f in range(tokens.shape[0] // FRAME):
        rows = pl.ds(f * FRAME, FRAME)
        live = flags[f * FRAME] > 0
        kept, other = keep[rows, :].astype(F32), got[rows, :].astype(F32)
        primal = jnp.where(is_second, other, kept)
        tangent = jnp.where(is_second, kept, other)
        base = tokens[rows, :].astype(F32)
        d_base = d_tokens[rows, :].astype(F32)
        d_base = jnp.where(live, d_base, jnp.zeros_like(d_base))
        result[rows, :] = (base + scale * primal).astype(BF)
        d_result[rows, :] = (d_base + scale * tangent).astype(BF)


def per_device(
    queries,
    d_queries,
    key_rows,
    value_rows,
    d_key_rows,
    d_value_rows,
    live_flags,
    out_weight,
    gate_scale,
    tokens,
    d_tokens,
):
    rows, width = queries.shape
    columns = tokens.shape[1]
    t, m = lax.axis_index("tm"), lax.axis_index("mp")
    odd = (t // NY % 2).astype(jnp.int32).reshape(1)
    core = (m % 2).astype(jnp.int32).reshape(1)
    half = (m // 2 % 2).astype(jnp.int32).reshape(1)
    x = m // 4

    def shape(r, c, dtype=BF):
        return jax.ShapeDtypeStruct((r, c), dtype)

    qd_own, qd_other, kv_own, kv_other = pl.pallas_call(
        pack_kernel,
        out_shape=[shape(rows, 2 * HD)] * 2 + [shape(rows, 4 * HD)] * 2,
        in_specs=[SMEM_SPEC] * 2 + [VMEM_SPEC] * 6,
        out_specs=[VMEM_SPEC] * 4,
        compiler_params=params(),
        name="pack",
    )(odd, live_flags, queries, d_queries, key_rows, value_rows, d_key_rows, d_value_rows)

    def z(a, k):
        return lax.ppermute(a, "tm", over_z(k))

    def y(a, k):
        return lax.ppermute(a, "tm", over_y(k))

    kv_got = z(kv_other, 1)
    kv = [kv_own] + [y(kv_own, k) for k in (1, 3, 2)]
    kv += [kv_got] + [y(kv_got, k) for k in (1, 3, 2)]
    qd = [qd_own] + [z(qd_other if k % 2 else qd_own, k) for k in range(1, 8)]

    part = shape(rows + STAT_ROWS, 2 * HD)
    parts = pl.pallas_call(
        functools.partial(attend_kernel, 2),
        out_shape=[part] * 8,
        in_specs=[ANY_SPEC] * 16,
        out_specs=[ANY_SPEC] * 8,
        scratch_shapes=[
            pltpu.VMEM((8 * rows, 4 * HD), BF),
            pltpu.VMEM((8 * rows, 2 * HD), BF),
            pltpu.VMEM((8, rows + STAT_ROWS, 2 * HD), BF),
            pltpu.SemaphoreType.DMA((16,)),
        ],
        compiler_params=params(),
        name="attend",
    )(*kv, *qd)
    parts = [parts[0]] + [z(parts[k], k) for k in range(1, 8)]

    group = 4 * columns
    w_own = []
    for k in range(4):
        piece = lax.dynamic_slice(out_weight, (0, (x + k) % NX * group), (width, group))
        w_own.append(lax.ppermute(piece, "mp", over_x(k)) if k else piece)
    w_other = [lax.ppermute(piece, "mp", over_core()) for piece in w_own]

    keep, send = pl.pallas_call(
        merge_kernel,
        out_shape=[shape(rows, 2 * HD)] * 2,
        in_specs=[SMEM_SPEC] + [VMEM_SPEC] * 8,
        out_specs=[VMEM_SPEC] * 2,
        compiler_params=params(),
        name="merge",
    )(jnp.concatenate([odd, core]), *parts)
    act = jnp.concatenate([keep, lax.ppermute(send, "mp", over_core())], axis=1)
    acts = [act] + [lax.ppermute(act, "mp", over_x(k)) for k in (1, 2, 3)]

    mine, theirs = pl.pallas_call(
        project_kernel,
        out_shape=[shape(rows, 2 * columns, F32), shape(rows, 2 * columns)],
        in_specs=[SMEM_SPEC] + [VMEM_SPEC] * 12,
        out_specs=[VMEM_SPEC] * 2,
        compiler_params=params(),
        name="project",
    )(half, *acts, *w_own, *w_other)
    theirs = lax.ppermute(theirs, "mp", over_half())

    keep, send = pl.pallas_call(
        add_kernel,
        out_shape=[shape(rows, columns)] * 2,
        in_specs=[SMEM_SPEC] + [VMEM_SPEC] * 2,
        out_specs=[VMEM_SPEC] * 2,
        compiler_params=params(),
        name="add",
    )(core, mine, theirs)
    got = lax.ppermute(send, "mp", over_core())

    result, d_result = pl.pallas_call(
        finish_kernel,
        out_shape=[shape(rows, columns)] * 2,
        in_specs=[SMEM_SPEC] * 2 + [VMEM_SPEC] * 5,
        out_specs=[VMEM_SPEC] * 2,
        compiler_params=params(),
        name="finish",
    )(core, live_flags, keep, got, gate_scale.reshape(1, columns), tokens, d_tokens)
    return (result, d_result)


def solution(mesh):
    placed = (
        P("tm", "mp"),
        P("tm", "mp"),
        P("tm", "mp"),
        P("tm", "mp"),
        P("tm", "mp"),
        P("tm", "mp"),
        P("tm"),
        P("mp", None),
        P("mp"),
        P("tm", "mp"),
        P("tm", "mp"),
    )
    return jax.shard_map(
        per_device,
        mesh=mesh,
        in_specs=placed,
        out_specs=(P("tm", "mp"), P("tm", "mp")),
        check_vma=False,
    )
```

```python
import functools
import math

import jax
import jax.numpy as jnp
from jax import lax
from jax.experimental import pallas as pl
from jax.experimental.pallas import tpu as pltpu
from jax.sharding import PartitionSpec as P

HD = 128
FRAME = 32
NZ, NY, NX = 8, 4, 4
FACTOR = 1.0 / math.sqrt(HD)
LOG2E = math.log2(math.e)
STAT_ROWS = 16
BF = jnp.bfloat16
F32 = jnp.float32
def params(mib):
    return pltpu.CompilerParams(vmem_limit_bytes=mib * 1024 * 1024)


SMEM_SPEC = pl.BlockSpec(memory_space=pltpu.SMEM)
VMEM_SPEC = pl.BlockSpec(memory_space=pltpu.VMEM)
HBM_SPEC = pl.BlockSpec(memory_space=pltpu.HBM)


def over_z(k):
    return [(z * NY + y, (z ^ k) * NY + y) for z in range(NZ) for y in range(NY)]


def over_y(k):
    return [(z * NY + y, z * NY + (y + k) % NY) for z in range(NZ) for y in range(NY)]


def over_x(k):
    return [(x * 4 + r, (x + k) % NX * 4 + r) for x in range(NX) for r in range(4)]


def flip(bits):
    return [(i, i ^ bits) for i in range(4 * NX)]


def same_y():
    return [[z * NY + y for z in range(NZ)] for y in range(NY)]


def pack_kernel(odd, flags, *refs):
    sources, (qd_out, kv_own, kv_other) = refs[:6], refs[6:9]
    held, qd, kv, other, sems = refs[9:15], refs[15:17], refs[17], refs[18], refs[19]
    rows_all = other.shape[0]
    copies = [pltpu.make_async_copy(sources[i], held[i], sems.at[i]) for i in range(6)]
    for copy in copies:
        copy.start()
    for copy in copies:
        copy.wait()
    q, dq, k, v, dk, dv = held
    is_odd = odd[0] > 0
    for f in range(rows_all // FRAME):
        rows = pl.ds(f * FRAME, FRAME)
        live = flags[f * FRAME] > 0

        def masked(ref):
            block = ref[rows, :]
            return jnp.where(live, block, jnp.zeros_like(block))

        for i, block in enumerate((masked(dq), q[rows, :])):
            for h in range(2):
                qd[h][rows, i * HD : (i + 1) * HD] = block[:, h * HD : (h + 1) * HD]
        for i, block in enumerate((k[rows, :], masked(dk), v[rows, :], masked(dv))):
            first, second = block[:, :HD], block[:, HD:]
            kv[rows, i * HD : (i + 1) * HD] = jnp.where(is_odd, second, first)
            other[rows, i * HD : (i + 1) * HD] = jnp.where(is_odd, first, second)
    copies = [
        pltpu.make_async_copy(other, kv_other, sems.at[0]),
        pltpu.make_async_copy(kv, kv_own.at[pl.ds(0, rows_all)], sems.at[1]),
    ]
    for i in range(NZ):
        at = pl.ds(i * rows_all, rows_all)
        copies.append(pltpu.make_async_copy(qd[i % 2], qd_out.at[at], sems.at[2 + i]))
    for copy in copies:
        copy.start()
    for copy in copies:
        copy.wait()


def join_kernel(at, got, own_in, own, sem):
    del own_in
    rows, width = got.shape
    copy = pltpu.make_async_copy(
        got, own.at[pl.ds(at * rows, rows), pl.ds((1 - at) * width, width)], sem
    )
    copy.start()
    copy.wait()


def in_three(value):
    high = value.astype(BF).astype(F32)
    middle = (value - high).astype(BF).astype(F32)
    low = (value - high - middle).astype(BF).astype(F32)
    return high, middle, low


def attend_kernel(*refs):
    kv_in, qd_in, out = refs[:4], refs[4], refs[5]
    kv, qd, held, sems = refs[6:]
    rows = kv_in[0].shape[0]
    half = rows // 2
    copies = [pltpu.make_async_copy(qd_in, qd, sems.at[4])]
    for i in range(4):
        copies.append(pltpu.make_async_copy(kv_in[i], kv.at[pl.ds(i * rows, rows)], sems.at[i]))
    for copy in copies:
        copy.start()
    for copy in copies:
        copy.wait()
    contract = (((1,), (1,)), ((), ()))

    def step(j, carry):
        both = qd[pl.ds(pl.multiple_of(j * rows, rows), rows), :]
        scores = lax.dot_general(both[:, HD:], kv[:, :HD], contract, preferred_element_type=F32)
        slopes = lax.dot_general(both, kv[:, : 2 * HD], contract, preferred_element_type=F32)
        scores = scores * (FACTOR * LOG2E)
        peak = jnp.max(scores, axis=1, keepdims=True)
        weights = jnp.exp2(scores - peak)
        total = jnp.sum(weights, axis=1, keepdims=True)
        product = weights * slopes
        slope = jnp.sum(product, axis=1, keepdims=True)
        weighted = jnp.dot(weights.astype(BF), kv[:, 2 * HD :], preferred_element_type=F32)
        tangent = jnp.dot(product.astype(BF), kv[:, 2 * HD : 3 * HD], preferred_element_type=F32)
        inverse = 1.0 / total
        mean = slope * (inverse * FACTOR)
        primal = weighted[:, :HD] * inverse
        tangent = (tangent * FACTOR + weighted[:, HD:]) * inverse - mean * primal
        lanes = lax.broadcasted_iota(jnp.int32, (rows, HD), 1)
        stats = jnp.zeros((rows, HD), F32)
        for i, part in enumerate(in_three(peak + jnp.log2(total)) + in_three(mean)):
            stats = jnp.where(lanes == i, part, stats)
        for p in range(2):
            mine = slice(p * half, (p + 1) * half)
            at = p * (half + STAT_ROWS)
            held[j, at : at + half, :HD] = primal[mine].astype(BF)
            held[j, at : at + half, HD:] = tangent[mine].astype(BF)
            tile = jnp.concatenate([stats[mine], jnp.zeros((2 * HD - half, HD), F32)], axis=0)
            held[j, at + half : at + half + STAT_ROWS, :] = tile.T[:STAT_ROWS].astype(BF)
        return carry

    lax.fori_loop(0, 4, step, 0)
    count = held.shape[1]
    back = [
        pltpu.make_async_copy(held.at[i], out.at[pl.ds(i * count, count)], sems.at[i])
        for i in range(4)
    ]
    for copy in back:
        copy.start()
    for copy in back:
        copy.wait()


def merge_kernel(core, parts, keep_all, send, keep, sem):
    rows = send.shape[0]
    step = rows + STAT_ROWS
    is_second = core[0] > 0
    tiles = [parts[i * step + rows : (i + 1) * step, :].astype(F32) for i in range(NZ)]
    stats = jnp.concatenate(tiles, axis=0).T[:rows]

    def value(i, first):
        lane = i * STAT_ROWS + first
        return sum(stats[:, lane + j : lane + j + 1] for j in range(3))

    for h in range(2):
        group = range(h, NZ, 2)
        sizes = [value(i, 0) for i in group]
        means = [value(i, 3) for i in group]
        peak = functools.reduce(jnp.maximum, sizes)
        sizes = [jnp.exp2(size - peak) for size in sizes]
        inverse = 1.0 / sum(sizes)
        sizes = [size * inverse for size in sizes]
        mean = sum(size * m for size, m in zip(sizes, means))
        primal = jnp.zeros((rows, HD), F32)
        tangent = jnp.zeros((rows, HD), F32)
        for i, size, m in zip(group, sizes, means):
            at = i * step
            a = parts[at : at + rows, :HD].astype(F32)
            primal += size * a
            tangent += size * parts[at : at + rows, HD:].astype(F32) + (size * (m - mean)) * a
        primal, tangent = primal.astype(BF), tangent.astype(BF)
        at = slice(h * HD, (h + 1) * HD)
        keep[:, at] = jnp.where(is_second, tangent, primal)
        send[:, at] = jnp.where(is_second, primal, tangent)
    copy = pltpu.make_async_copy(keep, keep_all.at[:, pl.ds(0, 2 * HD)], sem)
    copy.start()
    copy.wait()


def project_kernel(place, *refs):
    acts, w_own, w_other, (mine, others) = refs[:4], refs[4], refs[5], refs[6:]
    width = mine.shape[1]
    depth = w_own.shape[0] // 4
    is_second = place[1] > 0
    for half in range(2):

        @pl.when(place[0] == half)
        def _():
            at = slice(2 * half * width, 2 * (half + 1) * width)
            total = jnp.zeros((mine.shape[0], 2 * width), F32)
            for i in range(4):
                down = slice(i * depth, (i + 1) * depth)
                total += jnp.dot(acts[i][:, :depth], w_own[down, at], preferred_element_type=F32)
                total += jnp.dot(acts[i][:, depth:], w_other[down, at], preferred_element_type=F32)
            first, second = total[:, :width], total[:, width:]
            mine[...] = jnp.where(is_second, second, first).astype(mine.dtype)
            others[...] = jnp.where(is_second, first, second).astype(others.dtype)


def stack_kernel(*refs):
    pieces, out, sems = refs[:4], refs[4], refs[5]
    rows = pieces[0].shape[0]
    copies = [
        pltpu.make_async_copy(pieces[i], out.at[pl.ds(i * rows, rows)], sems.at[i])
        for i in range(4)
    ]
    for copy in copies:
        copy.start()
    for copy in copies:
        copy.wait()


def finish_kernel(
    core, flags, mine, z_got, core_got, both_got, gate, tokens, d_tokens, result, d_result
):
    is_second = core[0] > 0
    scale = gate[...]
    for f in range(tokens.shape[0] // FRAME):
        rows = pl.ds(f * FRAME, FRAME)
        live = flags[f * FRAME] > 0
        kept = mine[rows, :] + z_got[rows, :].astype(F32)
        other = core_got[rows, :].astype(F32) + both_got[rows, :].astype(F32)
        primal = jnp.where(is_second, other, kept)
        tangent = jnp.where(is_second, kept, other)
        base = tokens[rows, :].astype(F32)
        d_base = d_tokens[rows, :].astype(F32)
        d_base = jnp.where(live, d_base, jnp.zeros_like(d_base))
        result[rows, :] = (base + scale * primal).astype(BF)
        d_result[rows, :] = (d_base + scale * tangent).astype(BF)


def per_device(
    queries,
    d_queries,
    key_rows,
    value_rows,
    d_key_rows,
    d_value_rows,
    live_flags,
    out_weight,
    gate_scale,
    tokens,
    d_tokens,
):
    rows, width = queries.shape
    columns = tokens.shape[1]
    t, m = lax.axis_index("tm"), lax.axis_index("mp")
    odd = (t // NY % 2).astype(jnp.int32).reshape(1)
    core = (m % 2).astype(jnp.int32).reshape(1)
    half = (m // 2 % 2).astype(jnp.int32).reshape(1)
    x = m // 4

    def shape(r, c, dtype=BF):
        return jax.ShapeDtypeStruct((r, c), dtype)

    qd, kv, kv_other = pl.pallas_call(
        pack_kernel,
        out_shape=[shape(NZ * rows, 2 * HD), shape(2 * rows, 4 * HD), shape(rows, 4 * HD)],
        in_specs=[SMEM_SPEC] * 2 + [HBM_SPEC] * 6,
        out_specs=[HBM_SPEC] * 3,
        scratch_shapes=[pltpu.VMEM((rows, width), BF)] * 6
        + [pltpu.VMEM((rows, 2 * HD), BF)] * 2
        + [pltpu.VMEM((rows, 4 * HD), BF)] * 2
        + [pltpu.SemaphoreType.DMA((2 + NZ,))],
        compiler_params=params(60),
        name="pack",
    )(odd, live_flags, queries, d_queries, key_rows, value_rows, d_key_rows, d_value_rows)

    def join(got, own, at):
        return pl.pallas_call(
            functools.partial(join_kernel, at),
            out_shape=jax.ShapeDtypeStruct(own.shape, BF),
            in_specs=[HBM_SPEC] * 2,
            out_specs=HBM_SPEC,
            scratch_shapes=[pltpu.SemaphoreType.DMA],
            input_output_aliases={1: 0},
            compiler_params=params(8),
            name="join",
        )(got, own)

    def y(a, k):
        return lax.ppermute(a, "tm", over_y(k))

    def exchange(a):
        return lax.all_to_all(a, "tm", 0, 0, axis_index_groups=same_y(), tiled=True)

    group = 4 * columns
    qd, out_weight = lax.optimization_barrier((qd, out_weight))
    w_own = [
        lax.dynamic_slice(out_weight, (0, (x + k) % NX * group), (width, group)) for k in range(4)
    ]
    kv_got = lax.ppermute(kv_other, "tm", over_z(1))
    w_one, w_three = (lax.ppermute(w_own[k], "mp", over_x(k)) for k in (1, 3))
    qd, kv_got = lax.optimization_barrier((qd, kv_got))
    kv = join(kv_got, kv, 1)
    kv = [kv] + [y(kv, k) for k in (1, 3, 2)]
    w_two, kv[1] = lax.optimization_barrier((w_own[2], kv[1]))
    w_two = lax.ppermute(w_two, "mp", over_x(2))
    qd = exchange(qd)

    parts = pl.pallas_call(
        attend_kernel,
        out_shape=shape(NZ * (rows + STAT_ROWS), 2 * HD),
        in_specs=[HBM_SPEC] * 5,
        out_specs=HBM_SPEC,
        scratch_shapes=[
            pltpu.VMEM((NZ * rows, 4 * HD), BF),
            pltpu.VMEM((NZ * rows, 2 * HD), BF),
            pltpu.VMEM((4, 2 * (rows + STAT_ROWS), 2 * HD), BF),
            pltpu.SemaphoreType.DMA((5,)),
        ],
        compiler_params=params(24),
        name="attend",
    )(*kv, qd)
    w_own = [w_own[0], w_one, w_two, w_three]
    w_own, parts = lax.optimization_barrier((w_own, parts))
    parts = exchange(parts)

    act, send = pl.pallas_call(
        merge_kernel,
        out_shape=[shape(rows, 4 * HD), shape(rows, 2 * HD)],
        in_specs=[SMEM_SPEC, VMEM_SPEC],
        out_specs=[HBM_SPEC, VMEM_SPEC],
        scratch_shapes=[pltpu.VMEM((rows, 2 * HD), BF), pltpu.SemaphoreType.DMA],
        compiler_params=params(8),
        name="merge",
    )(core, parts)
    w_own = pl.pallas_call(
        stack_kernel,
        out_shape=shape(4 * width, group),
        in_specs=[HBM_SPEC] * 4,
        out_specs=HBM_SPEC,
        scratch_shapes=[pltpu.SemaphoreType.DMA((4,))],
        compiler_params=params(8),
        name="stack",
    )(*w_own)
    w_other = lax.ppermute(w_own, "mp", flip(1))
    act = join(lax.ppermute(send, "mp", flip(1)), act, 0)
    acts = [act] + [lax.ppermute(act, "mp", over_x(k)) for k in (1, 2, 3)]

    def project(which, dtype):
        return pl.pallas_call(
            project_kernel,
            out_shape=[shape(rows, columns, dtype), shape(rows, columns)],
            in_specs=[SMEM_SPEC] + [VMEM_SPEC] * 6,
            out_specs=[VMEM_SPEC] * 2,
            compiler_params=params(20),
            name="project",
        )(jnp.concatenate([which, core]), *acts, w_own, w_other)

    z_send, both_send = project(1 - half, BF)
    mine, core_send = project(half, F32)
    z_got = lax.ppermute(z_send, "mp", flip(2))
    both_got = lax.ppermute(both_send, "mp", flip(3))
    core_got = lax.ppermute(core_send, "mp", flip(1))

    result, d_result = pl.pallas_call(
        finish_kernel,
        out_shape=[shape(rows, columns)] * 2,
        in_specs=[SMEM_SPEC] * 2 + [VMEM_SPEC] * 7,
        out_specs=[VMEM_SPEC] * 2,
        compiler_params=params(8),
        name="finish",
    )(
        core,
        live_flags,
        mine,
        z_got,
        core_got,
        both_got,
        gate_scale.reshape(1, columns),
        tokens,
        d_tokens,
    )
    return (result, d_result)


def solution(mesh):
    placed = (
        P("tm", "mp"),
        P("tm", "mp"),
        P("tm", "mp"),
        P("tm", "mp"),
        P("tm", "mp"),
        P("tm", "mp"),
        P("tm"),
        P("mp", None),
        P("mp"),
        P("tm", "mp"),
        P("tm", "mp"),
    )
    return jax.shard_map(
        per_device,
        mesh=mesh,
        in_specs=placed,
        out_specs=(P("tm", "mp"), P("tm", "mp")),
        check_vma=False,
    )
```

```python
import functools
import math

import jax
import jax.numpy as jnp
from jax import lax
from jax.experimental import pallas as pl
from jax.experimental.pallas import tpu as pltpu
from jax.sharding import PartitionSpec as P

HD = 128
FRAME = 32
NZ, NY, NX = 8, 4, 4
FACTOR = 1.0 / math.sqrt(HD)
LOG2E = math.log2(math.e)
STAT_ROWS = 16
BF = jnp.bfloat16
F32 = jnp.float32
def params(mib):
    return pltpu.CompilerParams(vmem_limit_bytes=mib * 1024 * 1024)


SMEM_SPEC = pl.BlockSpec(memory_space=pltpu.SMEM)
VMEM_SPEC = pl.BlockSpec(memory_space=pltpu.VMEM)
HBM_SPEC = pl.BlockSpec(memory_space=pltpu.HBM)


def over_z(k):
    return [(z * NY + y, (z ^ k) * NY + y) for z in range(NZ) for y in range(NY)]


def over_y(k):
    return [(z * NY + y, z * NY + (y + k) % NY) for z in range(NZ) for y in range(NY)]


def flip(bits):
    return [(i, i ^ bits) for i in range(4 * NX)]


def same_y():
    return [[z * NY + y for z in range(NZ)] for y in range(NY)]


def over_x(k):
    return [(x * 4 + r, (x + k) % NX * 4 + r) for x in range(NX) for r in range(4)]


def over_x_and_core():
    return [[x * 4 + h * 2 + c for x in range(NX) for c in range(2)] for h in range(2)]


def over_half_and_core():
    return [[x * 4 + r for r in range(4)] for x in range(NX)]


def load(sources, held, sems):
    copies = [pltpu.make_async_copy(a, b, sems.at[i]) for i, (a, b) in enumerate(zip(sources, held))]
    for copy in copies:
        copy.start()
    for copy in copies:
        copy.wait()


def run_all(copies):
    for copy in copies:
        copy.start()
    for copy in copies:
        copy.wait()


def masked_rows(flags, f, ref):
    block = ref[pl.ds(f * FRAME, FRAME), :]
    return jnp.where(flags[f * FRAME] > 0, block, jnp.zeros_like(block))


def pack_keys_kernel(odd, flags, *refs):
    sources, (kv_own, kv_other), held, (kv, other, sems) = refs[:4], refs[4:6], refs[6:10], refs[10:]
    load(sources, held, sems)
    k, v, dk, dv = held
    is_odd = odd[0] > 0
    rows_all = other.shape[0]
    for f in range(rows_all // FRAME):
        rows = pl.ds(f * FRAME, FRAME)
        blocks = (k[rows, :], masked_rows(flags, f, dk), v[rows, :], masked_rows(flags, f, dv))
        for i, block in enumerate(blocks):
            first, second = block[:, :HD], block[:, HD:]
            kv[rows, i * HD : (i + 1) * HD] = jnp.where(is_odd, second, first)
            other[rows, i * HD : (i + 1) * HD] = jnp.where(is_odd, first, second)
    run_all(
        [
            pltpu.make_async_copy(other, kv_other, sems.at[0]),
            pltpu.make_async_copy(kv, kv_own.at[pl.ds(0, rows_all)], sems.at[1]),
        ]
    )


def pack_queries_kernel(flags, q_in, dq_in, qd_out, q, dq, first, second, sems):
    load((q_in, dq_in), (q, dq), sems)
    rows_all = q.shape[0]
    for f in range(rows_all // FRAME):
        rows = pl.ds(f * FRAME, FRAME)
        for i, block in enumerate((masked_rows(flags, f, dq), q[rows, :])):
            first[rows, i * HD : (i + 1) * HD] = block[:, :HD]
            second[rows, i * HD : (i + 1) * HD] = block[:, HD:]
    run_all(
        [
            pltpu.make_async_copy(
                second if i % 2 else first, qd_out.at[pl.ds(i * rows_all, rows_all)], sems.at[i]
            )
            for i in range(NZ)
        ]
    )


def join_kernel(got, own_in, own, sem):
    del own_in
    rows = got.shape[0]
    copy = pltpu.make_async_copy(got, own.at[pl.ds(rows, rows)], sem)
    copy.start()
    copy.wait()


def in_three(value):
    high = value.astype(BF).astype(F32)
    middle = (value - high).astype(BF).astype(F32)
    low = (value - high - middle).astype(BF).astype(F32)
    return high, middle, low


def attend_kernel(*refs):
    kv_in, qd_in, out = refs[:4], refs[4], refs[5]
    kv, qd, held, sems = refs[6:]
    rows = kv_in[0].shape[0]
    run_all(
        [
            pltpu.make_async_copy(kv_in[i], kv.at[pl.ds(i * rows, rows)], sems.at[i])
            for i in range(4)
        ]
        + [pltpu.make_async_copy(qd_in, qd, sems.at[4])]
    )
    contract = (((1,), (1,)), ((), ()))
    steps = qd.shape[0] // rows
    blocks = NZ // steps
    block = rows // blocks

    for j in range(steps):
        both = qd[j * rows : (j + 1) * rows, :]
        scores = lax.dot_general(both[:, HD:], kv[:, :HD], contract, preferred_element_type=F32)
        slopes = lax.dot_general(both, kv[:, : 2 * HD], contract, preferred_element_type=F32)
        peak = jnp.max(scores, axis=1, keepdims=True) * (FACTOR * LOG2E)
        weights = jnp.exp2(scores * (FACTOR * LOG2E) - peak)
        total = jnp.sum(weights, axis=1, keepdims=True)
        product = weights * slopes
        slope = jnp.sum(product, axis=1, keepdims=True)
        weighted = jnp.dot(weights.astype(BF), kv[:, 2 * HD :], preferred_element_type=F32)
        tangent = jnp.dot(product.astype(BF), kv[:, 2 * HD : 3 * HD], preferred_element_type=F32)
        inverse = 1.0 / total
        mean = slope * (inverse * FACTOR)
        primal = weighted[:, :HD] * inverse
        tangent = (tangent * FACTOR + weighted[:, HD:]) * inverse - mean * primal
        lanes = lax.broadcasted_iota(jnp.int32, (rows, HD), 1)
        stats = jnp.zeros((rows, HD), F32)
        for i, part in enumerate(in_three(peak + jnp.log2(total)) + in_three(mean)):
            stats = jnp.where(lanes == i, part, stats)
        for p in range(blocks):
            mine = slice(p * block, (p + 1) * block)
            at = p * (block + STAT_ROWS)
            held[j, at : at + block, :HD] = primal[mine].astype(BF)
            held[j, at : at + block, HD:] = tangent[mine].astype(BF)
            tile = jnp.concatenate([stats[mine], jnp.zeros((2 * HD - block, HD), F32)], axis=0)
            held[j, at + block : at + block + STAT_ROWS, :] = tile.T[:STAT_ROWS].astype(BF)
    count = held.shape[1]
    run_all(
        [
            pltpu.make_async_copy(held.at[i], out.at[pl.ds(i * count, count)], sems.at[i])
            for i in range(steps)
        ]
    )


def merge_kernel(parts, out, merged, sems):
    rows = merged.shape[1]
    step = rows + STAT_ROWS
    tiles = [parts[i * step + rows : (i + 1) * step, :].astype(F32) for i in range(NZ)]
    stats = jnp.concatenate(tiles, axis=0).T[:rows]

    def value(i, first):
        lane = i * STAT_ROWS + first
        return sum(stats[:, lane + j : lane + j + 1] for j in range(3))

    for h in range(2):
        group = range(h, NZ, 2)
        sizes = [value(i, 0) for i in group]
        means = [value(i, 3) for i in group]
        peak = functools.reduce(jnp.maximum, sizes)
        sizes = [jnp.exp2(size - peak) for size in sizes]
        inverse = 1.0 / sum(sizes)
        sizes = [size * inverse for size in sizes]
        mean = sum(size * m for size, m in zip(sizes, means))
        primal = jnp.zeros((rows, HD), F32)
        tangent = jnp.zeros((rows, HD), F32)
        for i, size, m in zip(group, sizes, means):
            at = i * step
            a = parts[at : at + rows, :HD].astype(F32)
            primal += size * a
            tangent += size * parts[at : at + rows, HD:].astype(F32) + (size * (m - mean)) * a
        at = slice(h * HD, (h + 1) * HD)
        merged[0, :, at] = primal.astype(BF)
        merged[1, :, at] = tangent.astype(BF)
    run_all(
        [pltpu.make_async_copy(merged, out.at[pl.ds(2 * i, 2)], sems.at[i]) for i in range(NX)]
    )


def stack_kernel(*refs):
    pieces, out, sems = refs[:NX], refs[NX], refs[NX + 1]
    run_all([pltpu.make_async_copy(pieces[i], out.at[i], sems.at[i]) for i in range(NX)])


def project_kernel(place, acts, w_own, w_other, out):
    width = out.shape[2]
    core, x = place[0], place[1]
    for half in range(2):
        columns = slice(2 * half * width, 2 * (half + 1) * width)
        total = jnp.zeros((out.shape[1], 2 * width), F32)
        for k in range(NX):
            i = 2 * lax.rem(x + NX - k, NX)
            total += jnp.dot(acts[i + core], w_own[k, :, columns], preferred_element_type=F32)
            total += jnp.dot(acts[i + 1 - core], w_other[k, :, columns], preferred_element_type=F32)
        out[2 * half] = total[:, :width].astype(BF)
        out[2 * half + 1] = total[:, width:].astype(BF)


def finish_kernel(flags, got, gate, tokens, d_tokens, result, d_result):
    scale = gate[...]
    for f in range(tokens.shape[0] // FRAME):
        rows = pl.ds(f * FRAME, FRAME)
        live = flags[f * FRAME] > 0
        primal = got[0, rows, :].astype(F32) + got[2, rows, :].astype(F32)
        tangent = got[1, rows, :].astype(F32) + got[3, rows, :].astype(F32)
        base = tokens[rows, :].astype(F32)
        d_base = d_tokens[rows, :].astype(F32)
        d_base = jnp.where(live, d_base, jnp.zeros_like(d_base))
        result[rows, :] = (base + scale * primal).astype(BF)
        d_result[rows, :] = (d_base + scale * tangent).astype(BF)


def per_device(
    queries,
    d_queries,
    key_rows,
    value_rows,
    d_key_rows,
    d_value_rows,
    live_flags,
    out_weight,
    gate_scale,
    tokens,
    d_tokens,
):
    rows, width = queries.shape
    columns = tokens.shape[1]
    t, m = lax.axis_index("tm"), lax.axis_index("mp")
    odd = (t // NY % 2).astype(jnp.int32).reshape(1)
    core = (m % 2).astype(jnp.int32).reshape(1)
    x = (m // 4).astype(jnp.int32).reshape(1)
    group = 4 * columns

    def shape(*dims):
        return jax.ShapeDtypeStruct(dims, BF)

    def after(a, b):
        return lax.optimization_barrier((a, b))[0]

    def exchange(a, axis, groups):
        return lax.all_to_all(a, axis, 0, 0, axis_index_groups=groups, tiled=True)

    def y(a, k):
        return lax.ppermute(a, "tm", over_y(k))

    kv, kv_other = pl.pallas_call(
        pack_keys_kernel,
        out_shape=[shape(2 * rows, 4 * HD), shape(rows, 4 * HD)],
        in_specs=[SMEM_SPEC] * 2 + [HBM_SPEC] * 4,
        out_specs=[HBM_SPEC] * 2,
        scratch_shapes=[pltpu.VMEM((rows, width), BF)] * 4
        + [pltpu.VMEM((rows, 4 * HD), BF)] * 2
        + [pltpu.SemaphoreType.DMA((4,))],
        compiler_params=params(60),
        name="pack_keys",
    )(odd, live_flags, key_rows, value_rows, d_key_rows, d_value_rows)
    kv_got = lax.ppermute(kv_other, "tm", over_z(1))

    queries, out_weight = after((queries, out_weight), kv)
    weights = [
        lax.dynamic_slice(out_weight, (0, (x[0] + k) % NX * group), (width, group))
        for k in range(NX)
    ]
    qd = pl.pallas_call(
        pack_queries_kernel,
        out_shape=shape(NZ * rows, 2 * HD),
        in_specs=[SMEM_SPEC] + [HBM_SPEC] * 2,
        out_specs=HBM_SPEC,
        scratch_shapes=[pltpu.VMEM((rows, width), BF)] * 2
        + [pltpu.VMEM((rows, 2 * HD), BF)] * 2
        + [pltpu.SemaphoreType.DMA((NZ,))],
        compiler_params=params(60),
        name="pack_queries",
    )(live_flags, queries, d_queries)
    qd, kv_got = lax.optimization_barrier((qd, kv_got))
    qd = exchange(qd, "tm", same_y())

    kv = pl.pallas_call(
        join_kernel,
        out_shape=shape(2 * rows, 4 * HD),
        in_specs=[HBM_SPEC] * 2,
        out_specs=HBM_SPEC,
        scratch_shapes=[pltpu.SemaphoreType.DMA],
        input_output_aliases={1: 0},
        compiler_params=params(8),
        name="join",
    )(kv_got, kv)
    weights = after(weights, kv)
    kv = [kv] + [y(kv, k) for k in (1, 3, 2)]

    for k in (1, 3):
        weights[k] = lax.ppermute(weights[k], "mp", over_x(k))
    qd = after(qd, weights)

    parts = pl.pallas_call(
        attend_kernel,
        out_shape=shape(NZ * (rows + STAT_ROWS), 2 * HD),
        in_specs=[HBM_SPEC] * 5,
        out_specs=HBM_SPEC,
        scratch_shapes=[
            pltpu.VMEM((NZ * rows, 4 * HD), BF),
            pltpu.VMEM((NZ * rows, 2 * HD), BF),
            pltpu.VMEM((4, 2 * (rows + STAT_ROWS), 2 * HD), BF),
            pltpu.SemaphoreType.DMA((5,)),
        ],
        compiler_params=params(60),
        name="attend",
    )(*kv, qd)
    weights[2] = lax.ppermute(after(weights[2], parts), "mp", over_x(2))
    parts = exchange(parts, "tm", same_y())

    w_own = pl.pallas_call(
        stack_kernel,
        out_shape=shape(NX, width, group),
        in_specs=[HBM_SPEC] * NX,
        out_specs=HBM_SPEC,
        scratch_shapes=[pltpu.SemaphoreType.DMA((NX,))],
        compiler_params=params(8),
        name="stack",
    )(*weights)
    w_other = lax.ppermute(w_own, "mp", flip(1))

    acts = pl.pallas_call(
        merge_kernel,
        out_shape=shape(2 * NX, rows, 2 * HD),
        in_specs=[VMEM_SPEC],
        out_specs=HBM_SPEC,
        scratch_shapes=[pltpu.VMEM((2, rows, 2 * HD), BF), pltpu.SemaphoreType.DMA((NX,))],
        compiler_params=params(60),
        name="merge",
    )(parts)
    acts = exchange(acts, "mp", over_x_and_core())

    sums = pl.pallas_call(
        project_kernel,
        out_shape=shape(4, rows, columns),
        in_specs=[SMEM_SPEC] + [VMEM_SPEC] * 3,
        out_specs=VMEM_SPEC,
        compiler_params=params(24),
        name="project",
    )(jnp.concatenate([core, x]), acts, w_own, w_other)
    got = exchange(sums, "mp", over_half_and_core())

    result, d_result = pl.pallas_call(
        finish_kernel,
        out_shape=[shape(rows, columns)] * 2,
        in_specs=[SMEM_SPEC] + [VMEM_SPEC] * 4,
        out_specs=[VMEM_SPEC] * 2,
        compiler_params=params(8),
        name="finish",
    )(live_flags, got, gate_scale.reshape(1, columns), tokens, d_tokens)
    return (result, d_result)


def solution(mesh):
    placed = (
        P("tm", "mp"),
        P("tm", "mp"),
        P("tm", "mp"),
        P("tm", "mp"),
        P("tm", "mp"),
        P("tm", "mp"),
        P("tm"),
        P("mp", None),
        P("mp"),
        P("tm", "mp"),
        P("tm", "mp"),
    )
    return jax.shard_map(
        per_device,
        mesh=mesh,
        in_specs=placed,
        out_specs=(P("tm", "mp"), P("tm", "mp")),
        check_vma=False,
    )
```

```python
import functools
import math

import jax
import jax.numpy as jnp
from jax import lax
from jax.experimental import pallas as pl
from jax.experimental.pallas import tpu as pltpu
from jax.sharding import Mesh
from jax.sharding import PartitionSpec as P

HD = 128
FRAME = 32
NZ, NY, NX = 8, 4, 4
TM, MP = ("z", "z0", "y"), ("x", "half", "core")
FACTOR = 1.0 / math.sqrt(HD)
LOG2E = math.log2(math.e)
STAT_ROWS = 16
BF = jnp.bfloat16
F32 = jnp.float32
def params(mib):
    return pltpu.CompilerParams(vmem_limit_bytes=mib * 1024 * 1024)


SMEM_SPEC = pl.BlockSpec(memory_space=pltpu.SMEM)
VMEM_SPEC = pl.BlockSpec(memory_space=pltpu.VMEM)
HBM_SPEC = pl.BlockSpec(memory_space=pltpu.HBM)


def over_z(k):
    return [(z * NY + y, (z ^ k) * NY + y) for z in range(NZ) for y in range(NY)]


def over_y(k):
    return [(z * NY + y, z * NY + (y + k) % NY) for z in range(NZ) for y in range(NY)]


def flip(bits):
    return [(i, i ^ bits) for i in range(4 * NX)]


def load(sources, held, sems):
    copies = [pltpu.make_async_copy(a, b, sems.at[i]) for i, (a, b) in enumerate(zip(sources, held))]
    for copy in copies:
        copy.start()
    for copy in copies:
        copy.wait()


def run_all(copies):
    for copy in copies:
        copy.start()
    for copy in copies:
        copy.wait()


def masked_rows(flags, f, ref):
    block = ref[pl.ds(f * FRAME, FRAME), :]
    return jnp.where(flags[f * FRAME] > 0, block, jnp.zeros_like(block))


def pack_kernel(odd, flags, *refs):
    sources, (qd_own, kv_own, other_head), held = refs[:6], refs[6:9], refs[9:15]
    qd, kv, other, sems = refs[15:]
    load(sources, held, sems)
    q, dq, k, v, dk, dv = held
    is_odd = odd[0] > 0
    rows_all = other.shape[0]
    for f in range(rows_all // FRAME):
        rows = pl.ds(f * FRAME, FRAME)
        blocks = (
            masked_rows(flags, f, dq),
            q[rows, :],
            k[rows, :],
            masked_rows(flags, f, dk),
            v[rows, :],
            masked_rows(flags, f, dv),
        )
        for i, block in enumerate(blocks):
            first, second = block[:, :HD], block[:, HD:]
            own = jnp.where(is_odd, second, first)
            other[rows, i * HD : (i + 1) * HD] = jnp.where(is_odd, first, second)
            if i < 2:
                qd[rows, i * HD : (i + 1) * HD] = own
            else:
                kv[rows, (i - 2) * HD : (i - 1) * HD] = own
    top = pl.ds(0, rows_all)
    run_all(
        [
            pltpu.make_async_copy(other, other_head, sems.at[0]),
            pltpu.make_async_copy(qd, qd_own.at[top], sems.at[1]),
            pltpu.make_async_copy(kv, kv_own.at[top], sems.at[2]),
        ]
    )


def join_kernel(got, qd_in, kv_in, qd, kv, held, sems):
    del qd_in, kv_in
    rows = got.shape[0]
    below = pl.ds(rows, rows)
    run_all([pltpu.make_async_copy(got, held, sems.at[0])])
    run_all(
        [
            pltpu.make_async_copy(held.at[:, pl.ds(0, 2 * HD)], qd.at[below], sems.at[0]),
            pltpu.make_async_copy(held.at[:, pl.ds(2 * HD, 4 * HD)], kv.at[below], sems.at[1]),
        ]
    )


def cut_kernel(w_in, w_out, held, sems):
    group = w_out.shape[2]
    run_all([pltpu.make_async_copy(w_in, held, sems.at[0])])
    run_all(
        [
            pltpu.make_async_copy(held.at[:, pl.ds(i * group, group)], w_out.at[i], sems.at[i])
            for i in range(NX)
        ]
    )


def in_three(value):
    high = value.astype(BF).astype(F32)
    middle = (value - high).astype(BF).astype(F32)
    low = (value - high - middle).astype(BF).astype(F32)
    return high, middle, low


def attend_kernel(*refs):
    kv_in, qd_in, out = refs[:8], refs[8], refs[9]
    kv, qd, held, sems = refs[10:]
    rows = kv_in[0].shape[0]
    half = rows // 2
    run_all(
        [
            pltpu.make_async_copy(kv_in[i], kv.at[pl.ds(i * rows, rows)], sems.at[i])
            for i in range(8)
        ]
        + [pltpu.make_async_copy(qd_in, qd, sems.at[8])]
    )
    contract = (((1,), (1,)), ((), ()))
    both = qd[...]
    scores = lax.dot_general(both[:, HD:], kv[:, :HD], contract, preferred_element_type=F32)
    slopes = lax.dot_general(both, kv[:, : 2 * HD], contract, preferred_element_type=F32)
    peak = jnp.max(scores, axis=1, keepdims=True) * (FACTOR * LOG2E)
    weights = jnp.exp2(scores * (FACTOR * LOG2E) - peak)
    total = jnp.sum(weights, axis=1, keepdims=True)
    product = weights * slopes
    slope = jnp.sum(product, axis=1, keepdims=True)
    weighted = jnp.dot(weights.astype(BF), kv[:, 2 * HD :], preferred_element_type=F32)
    tangent = jnp.dot(product.astype(BF), kv[:, 2 * HD : 3 * HD], preferred_element_type=F32)
    inverse = 1.0 / total
    mean = slope * (inverse * FACTOR)
    primal = weighted[:, :HD] * inverse
    tangent = (tangent * FACTOR + weighted[:, HD:]) * inverse - mean * primal
    lanes = lax.broadcasted_iota(jnp.int32, (rows, HD), 1)
    stats = jnp.zeros((rows, HD), F32)
    for i, part in enumerate(in_three(peak + jnp.log2(total)) + in_three(mean)):
        stats = jnp.where(lanes == i, part, stats)
    for p in range(2):
        mine = slice(p * half, (p + 1) * half)
        at = p * (half + STAT_ROWS)
        held[at : at + half, :HD] = primal[mine].astype(BF)
        held[at : at + half, HD:] = tangent[mine].astype(BF)
        tile = jnp.concatenate([stats[mine], jnp.zeros((2 * HD - half, HD), F32)], axis=0)
        held[at + half : at + half + STAT_ROWS, :] = tile.T[:STAT_ROWS].astype(BF)
    run_all([pltpu.make_async_copy(held, out, sems.at[0])])


def merge_kernel(odd, one, two, out, merged, sems):
    rows = merged.shape[2]
    parts = (one, two)
    is_odd = odd[0] > 0
    found = []
    for p in range(2):
        at = p * (rows + STAT_ROWS)
        tiles = [part[at + rows : at + rows + STAT_ROWS, :].astype(F32) for part in parts]
        stats = jnp.concatenate(tiles * 4, axis=0).T[:rows]

        def value(i, first):
            lane = i * STAT_ROWS + first
            return sum(stats[:, lane + j : lane + j + 1] for j in range(3))

        sizes = [value(i, 0) for i in range(2)]
        means = [value(i, 3) for i in range(2)]
        peak = jnp.maximum(*sizes)
        sizes = [jnp.exp2(size - peak) for size in sizes]
        inverse = 1.0 / sum(sizes)
        sizes = [size * inverse for size in sizes]
        mean = sum(size * m for size, m in zip(sizes, means))
        primal = jnp.zeros((rows, HD), F32)
        tangent = jnp.zeros((rows, HD), F32)
        for part, size, m in zip(parts, sizes, means):
            a = part[at : at + rows, :HD].astype(F32)
            primal += size * a
            tangent += size * part[at : at + rows, HD:].astype(F32) + (size * (m - mean)) * a
        found.append((primal.astype(BF), tangent.astype(BF)))
    for kind in range(2):
        own, other = found[0][kind], found[1][kind]
        merged[0, kind] = jnp.where(is_odd, other, own)
        merged[1, kind] = jnp.where(is_odd, own, other)
    copies = []
    for parity in range(2):
        for i in range(NX):
            j = parity * NX + i
            copies.append(
                pltpu.make_async_copy(merged.at[parity], out.at[pl.ds(2 * j, 2)], sems.at[j])
            )
    run_all(copies)


def project_kernel(place, acts, w_own, w_other, mine, others):
    width = mine.shape[1]
    c = place[1]
    for half in range(2):

        @pl.when(place[0] == half)
        def _():
            columns = slice(2 * half * width, 2 * (half + 1) * width)
            total = jnp.zeros((mine.shape[0], 2 * width), F32)
            for k in range(NX):
                for w, i in ((w_own, 2 * k + c), (w_other, 2 * k + 1 - c)):
                    heads = jnp.concatenate([acts[i], acts[2 * NX + i]], axis=1)
                    total += jnp.dot(heads, w[k, :, columns], preferred_element_type=F32)
            first, second = total[:, :width], total[:, width:]
            mine[...] = jnp.where(c > 0, second, first).astype(mine.dtype)
            others[...] = jnp.where(c > 0, first, second).astype(others.dtype)


def finish_kernel(
    core, flags, mine, z_got, core_got, both_got, gate, tokens, d_tokens, result, d_result
):
    is_second = core[0] > 0
    scale = gate[...]
    for f in range(tokens.shape[0] // FRAME):
        rows = pl.ds(f * FRAME, FRAME)
        live = flags[f * FRAME] > 0
        kept = mine[rows, :] + z_got[rows, :].astype(F32)
        other = core_got[rows, :].astype(F32) + both_got[rows, :].astype(F32)
        primal = jnp.where(is_second, other, kept)
        tangent = jnp.where(is_second, kept, other)
        base = tokens[rows, :].astype(F32)
        d_base = d_tokens[rows, :].astype(F32)
        d_base = jnp.where(live, d_base, jnp.zeros_like(d_base))
        result[rows, :] = (base + scale * primal).astype(BF)
        d_result[rows, :] = (d_base + scale * tangent).astype(BF)


def per_device(
    queries,
    d_queries,
    key_rows,
    value_rows,
    d_key_rows,
    d_value_rows,
    live_flags,
    out_weight,
    gate_scale,
    tokens,
    d_tokens,
):
    rows, width = queries.shape
    columns = tokens.shape[1]
    t, m = lax.axis_index(TM), lax.axis_index(MP)
    odd = (t // NY % 2).astype(jnp.int32).reshape(1)
    core = (m % 2).astype(jnp.int32).reshape(1)
    group = 4 * columns

    def shape(*dims):
        return jax.ShapeDtypeStruct(dims, BF)

    def after(a, b):
        return lax.optimization_barrier((a, b))[0]

    def exchange(a, axes):
        return lax.all_to_all(a, axes, 0, 0, tiled=True)

    def y(a, k):
        return lax.ppermute(a, TM, over_y(k))

    def z(a, k):
        return lax.ppermute(a, TM, over_z(k))

    qd, kv, other_head = pl.pallas_call(
        pack_kernel,
        out_shape=[shape(2 * rows, 2 * HD), shape(2 * rows, 4 * HD), shape(rows, 6 * HD)],
        in_specs=[SMEM_SPEC] * 2 + [HBM_SPEC] * 6,
        out_specs=[HBM_SPEC] * 3,
        scratch_shapes=[pltpu.VMEM((rows, width), BF)] * 6
        + [
            pltpu.VMEM((rows, 2 * HD), BF),
            pltpu.VMEM((rows, 4 * HD), BF),
            pltpu.VMEM((rows, 6 * HD), BF),
            pltpu.SemaphoreType.DMA((6,)),
        ],
        compiler_params=params(60),
        name="pack",
    )(odd, live_flags, queries, d_queries, key_rows, value_rows, d_key_rows, d_value_rows)
    weights = pl.pallas_call(
        cut_kernel,
        out_shape=shape(NX, width, group),
        in_specs=[HBM_SPEC],
        out_specs=HBM_SPEC,
        scratch_shapes=[pltpu.VMEM(out_weight.shape, BF), pltpu.SemaphoreType.DMA((NX,))],
        compiler_params=params(60),
        name="cut",
    )(after(out_weight, kv))
    got = z(other_head, 1)
    got = after(got, weights)
    qd, kv = pl.pallas_call(
        join_kernel,
        out_shape=[shape(2 * rows, 2 * HD), shape(2 * rows, 4 * HD)],
        in_specs=[HBM_SPEC] * 3,
        out_specs=[HBM_SPEC] * 2,
        scratch_shapes=[pltpu.VMEM((rows, 6 * HD), BF), pltpu.SemaphoreType.DMA((2,))],
        input_output_aliases={1: 0, 2: 1},
        compiler_params=params(60),
        name="join",
    )(got, qd, kv)
    kv_far = z(kv, 2)
    qd_far = z(qd, 4)
    kv = [kv] + [y(kv, k) for k in (1, 3, 2)] + [kv_far] + [y(kv_far, k) for k in (1, 3, 2)]

    w_own = exchange(after(weights, got), "x")
    qd_far = after(qd_far, w_own)

    def attend(piece):
        part = shape(2 * (rows + STAT_ROWS), 2 * HD)
        return pl.pallas_call(
            attend_kernel,
            out_shape=part,
            in_specs=[HBM_SPEC] * 9,
            out_specs=HBM_SPEC,
            scratch_shapes=[
                pltpu.VMEM((16 * rows, 4 * HD), BF),
                pltpu.VMEM((2 * rows, 2 * HD), BF),
                pltpu.VMEM(part.shape, BF),
                pltpu.SemaphoreType.DMA((9,)),
            ],
            compiler_params=params(60),
            name="attend",
        )(*kv, piece)

    far = attend(qd_far)
    near = attend(after(qd, far))
    returned = z(far, 4)

    w_other = lax.ppermute(after(w_own, far), MP, flip(1))

    acts = pl.pallas_call(
        merge_kernel,
        out_shape=shape(4 * NX, rows, HD),
        in_specs=[SMEM_SPEC] + [VMEM_SPEC] * 2,
        out_specs=HBM_SPEC,
        scratch_shapes=[pltpu.VMEM((2, 2, rows, HD), BF), pltpu.SemaphoreType.DMA((2 * NX,))],
        compiler_params=params(60),
        name="merge",
    )(odd, near, returned)
    acts = exchange(acts, ("z0", "x", "core"))

    half = (m // 2 % 2).astype(jnp.int32).reshape(1)

    def project(which, dtype):
        return pl.pallas_call(
            project_kernel,
            out_shape=[jax.ShapeDtypeStruct((rows, columns), dtype), shape(rows, columns)],
            in_specs=[SMEM_SPEC] + [VMEM_SPEC] * 3,
            out_specs=[VMEM_SPEC] * 2,
            compiler_params=params(24),
            name="project",
        )(jnp.concatenate([which, core]), acts, w_own, w_other)

    z_send, both_send = project(1 - half, BF)
    mine, core_send = project(half, F32)
    z_got = lax.ppermute(z_send, MP, flip(2))
    both_got = lax.ppermute(both_send, MP, flip(3))
    core_got = lax.ppermute(core_send, MP, flip(1))

    result, d_result = pl.pallas_call(
        finish_kernel,
        out_shape=[shape(rows, columns)] * 2,
        in_specs=[SMEM_SPEC] * 2 + [VMEM_SPEC] * 7,
        out_specs=[VMEM_SPEC] * 2,
        compiler_params=params(8),
        name="finish",
    )(
        core,
        live_flags,
        mine,
        z_got,
        core_got,
        both_got,
        gate_scale.reshape(1, columns),
        tokens,
        d_tokens,
    )
    return (result, d_result)


def solution(mesh):
    parts = mesh.devices.reshape(NZ // 2, 2, NY, NX, 2, 2)
    placed = (
        P(TM, MP),
        P(TM, MP),
        P(TM, MP),
        P(TM, MP),
        P(TM, MP),
        P(TM, MP),
        P(TM),
        P(MP, None),
        P(MP),
        P(TM, MP),
        P(TM, MP),
    )
    return jax.shard_map(
        per_device,
        mesh=Mesh(parts, TM + MP),
        in_specs=placed,
        out_specs=(P(TM, MP), P(TM, MP)),
        check_vma=False,
    )
```

```python
import functools
import math

import jax
import jax.numpy as jnp
from jax import lax
from jax.experimental import pallas as pl
from jax.experimental.pallas import tpu as pltpu
from jax.sharding import Mesh
from jax.sharding import PartitionSpec as P

HD = 128
FRAME = 32
NZ, NY, NX = 8, 4, 4
TM, MP = ("z", "z0", "y"), ("x", "half", "core")
FACTOR = 1.0 / math.sqrt(HD)
LOG2E = math.log2(math.e)
STAT_ROWS = 16
BF = jnp.bfloat16
F32 = jnp.float32
def params(mib):
    return pltpu.CompilerParams(vmem_limit_bytes=mib * 1024 * 1024)


SMEM_SPEC = pl.BlockSpec(memory_space=pltpu.SMEM)
VMEM_SPEC = pl.BlockSpec(memory_space=pltpu.VMEM)
HBM_SPEC = pl.BlockSpec(memory_space=pltpu.HBM)


def over_z(k):
    return [(z * NY + y, (z ^ k) * NY + y) for z in range(NZ) for y in range(NY)]


def over_y(k):
    return [(z * NY + y, z * NY + (y + k) % NY) for z in range(NZ) for y in range(NY)]


def flip(bits):
    return [(i, i ^ bits) for i in range(4 * NX)]


def load(sources, held, sems):
    copies = [pltpu.make_async_copy(a, b, sems.at[i]) for i, (a, b) in enumerate(zip(sources, held))]
    for copy in copies:
        copy.start()
    for copy in copies:
        copy.wait()


def run_all(copies):
    for copy in copies:
        copy.start()
    for copy in copies:
        copy.wait()


def masked_rows(flags, f, ref):
    block = ref[pl.ds(f * FRAME, FRAME), :]
    return jnp.where(flags[f * FRAME] > 0, block, jnp.zeros_like(block))


def pack_kernel(odd, flags, *refs):
    sources, (qd_own, kv_own, other_head), held = refs[:6], refs[6:9], refs[9:15]
    qd, kv, other, sems = refs[15:]
    load(sources, held, sems)
    q, dq, k, v, dk, dv = held
    is_odd = odd[0] > 0
    rows_all = other.shape[0]
    for f in range(rows_all // FRAME):
        rows = pl.ds(f * FRAME, FRAME)
        blocks = (
            masked_rows(flags, f, dq),
            q[rows, :],
            k[rows, :],
            masked_rows(flags, f, dk),
            v[rows, :],
            masked_rows(flags, f, dv),
        )
        for i, block in enumerate(blocks):
            first, second = block[:, :HD], block[:, HD:]
            own = jnp.where(is_odd, second, first)
            other[rows, i * HD : (i + 1) * HD] = jnp.where(is_odd, first, second)
            if i < 2:
                qd[rows, i * HD : (i + 1) * HD] = own
            else:
                kv[rows, (i - 2) * HD : (i - 1) * HD] = own
    top = pl.ds(0, rows_all)
    run_all(
        [
            pltpu.make_async_copy(other, other_head, sems.at[0]),
            pltpu.make_async_copy(qd, qd_own.at[top], sems.at[1]),
            pltpu.make_async_copy(kv, kv_own.at[top], sems.at[2]),
        ]
    )


def join_kernel(got, qd_in, kv_in, qd, kv, held, sems):
    del qd_in, kv_in
    rows = got.shape[0]
    below = pl.ds(rows, rows)
    run_all([pltpu.make_async_copy(got, held, sems.at[0])])
    run_all(
        [
            pltpu.make_async_copy(held.at[:, pl.ds(0, 2 * HD)], qd.at[below], sems.at[0]),
            pltpu.make_async_copy(held.at[:, pl.ds(2 * HD, 4 * HD)], kv.at[below], sems.at[1]),
        ]
    )


def cut_kernel(w_in, w_out, held, sems):
    group = w_out.shape[2]
    run_all([pltpu.make_async_copy(w_in, held, sems.at[0])])
    run_all(
        [
            pltpu.make_async_copy(held.at[:, pl.ds(i * group, group)], w_out.at[i], sems.at[i])
            for i in range(NX)
        ]
    )


def in_three(value):
    high = value.astype(BF).astype(F32)
    middle = (value - high).astype(BF).astype(F32)
    low = (value - high - middle).astype(BF).astype(F32)
    return high, middle, low


def attend_kernel(*refs):
    kv_in, qd_in, out = refs[:8], refs[8], refs[9]
    kv, qd, held, sems = refs[10:]
    rows = kv_in[0].shape[0]
    half = rows // 2
    run_all(
        [
            pltpu.make_async_copy(kv_in[i], kv.at[pl.ds(i * rows, rows)], sems.at[i])
            for i in range(8)
        ]
        + [pltpu.make_async_copy(qd_in, qd, sems.at[8])]
    )
    contract = (((1,), (1,)), ((), ()))
    both = qd[...]
    scores = lax.dot_general(both[:, HD:], kv[:, :HD], contract, preferred_element_type=F32)
    slopes = lax.dot_general(both, kv[:, : 2 * HD], contract, preferred_element_type=F32)
    peak = jnp.max(scores, axis=1, keepdims=True) * (FACTOR * LOG2E)
    weights = jnp.exp2(scores * (FACTOR * LOG2E) - peak)
    total = jnp.sum(weights, axis=1, keepdims=True)
    product = weights * slopes
    slope = jnp.sum(product, axis=1, keepdims=True)
    weighted = jnp.dot(weights.astype(BF), kv[:, 2 * HD :], preferred_element_type=F32)
    tangent = jnp.dot(product.astype(BF), kv[:, 2 * HD : 3 * HD], preferred_element_type=F32)
    inverse = 1.0 / total
    mean = slope * (inverse * FACTOR)
    primal = weighted[:, :HD] * inverse
    tangent = (tangent * FACTOR + weighted[:, HD:]) * inverse - mean * primal
    lanes = lax.broadcasted_iota(jnp.int32, (rows, HD), 1)
    stats = jnp.zeros((rows, HD), F32)
    for i, part in enumerate(in_three(peak + jnp.log2(total)) + in_three(mean)):
        stats = jnp.where(lanes == i, part, stats)
    for p in range(2):
        mine = slice(p * half, (p + 1) * half)
        at = p * (half + STAT_ROWS)
        held[at : at + half, :HD] = primal[mine].astype(BF)
        held[at : at + half, HD:] = tangent[mine].astype(BF)
        tile = jnp.concatenate([stats[mine], jnp.zeros((2 * HD - half, HD), F32)], axis=0)
        held[at + half : at + half + STAT_ROWS, :] = tile.T[:STAT_ROWS].astype(BF)
    run_all([pltpu.make_async_copy(held, out, sems.at[0])])


def merge_kernel(odd, one, two, out, merged, sems):
    rows = merged.shape[2]
    parts = (one, two)
    is_odd = odd[0] > 0
    found = []
    for p in range(2):
        at = p * (rows + STAT_ROWS)
        tiles = [part[at + rows : at + rows + STAT_ROWS, :].astype(F32) for part in parts]
        stats = jnp.concatenate(tiles * 4, axis=0).T[:rows]

        def value(i, first):
            lane = i * STAT_ROWS + first
            return sum(stats[:, lane + j : lane + j + 1] for j in range(3))

        sizes = [value(i, 0) for i in range(2)]
        means = [value(i, 3) for i in range(2)]
        peak = jnp.maximum(*sizes)
        sizes = [jnp.exp2(size - peak) for size in sizes]
        inverse = 1.0 / sum(sizes)
        sizes = [size * inverse for size in sizes]
        mean = sum(size * m for size, m in zip(sizes, means))
        primal = jnp.zeros((rows, HD), F32)
        tangent = jnp.zeros((rows, HD), F32)
        for part, size, m in zip(parts, sizes, means):
            a = part[at : at + rows, :HD].astype(F32)
            primal += size * a
            tangent += size * part[at : at + rows, HD:].astype(F32) + (size * (m - mean)) * a
        found.append((primal.astype(BF), tangent.astype(BF)))
    for kind in range(2):
        own, other = found[0][kind], found[1][kind]
        merged[0, kind] = jnp.where(is_odd, other, own)
        merged[1, kind] = jnp.where(is_odd, own, other)
    copies = []
    for parity in range(2):
        for i in range(NX):
            j = parity * NX + i
            copies.append(
                pltpu.make_async_copy(merged.at[parity], out.at[pl.ds(2 * j, 2)], sems.at[j])
            )
    run_all(copies)


def project_kernel(place, acts, w_own, w_other, mine, others):
    width = mine.shape[1]
    c = place[1]
    for half in range(2):

        @pl.when(place[0] == half)
        def _():
            columns = slice(2 * half * width, 2 * (half + 1) * width)
            total = jnp.zeros((mine.shape[0], 2 * width), F32)
            for k in range(NX):
                for w, i in ((w_own, 2 * k + c), (w_other, 2 * k + 1 - c)):
                    heads = jnp.concatenate([acts[i], acts[2 * NX + i]], axis=1)
                    total += jnp.dot(heads, w[k, :, columns], preferred_element_type=F32)
            first, second = total[:, :width], total[:, width:]
            mine[...] = jnp.where(c > 0, second, first).astype(mine.dtype)
            others[...] = jnp.where(c > 0, first, second).astype(others.dtype)


def finish_kernel(
    core, flags, mine, z_got, core_got, both_got, gate, tokens, d_tokens, result, d_result
):
    is_second = core[0] > 0
    scale = gate[...]
    for f in range(tokens.shape[0] // FRAME):
        rows = pl.ds(f * FRAME, FRAME)
        live = flags[f * FRAME] > 0
        kept = mine[rows, :] + z_got[rows, :].astype(F32)
        other = core_got[rows, :].astype(F32) + both_got[rows, :].astype(F32)
        primal = jnp.where(is_second, other, kept)
        tangent = jnp.where(is_second, kept, other)
        base = tokens[rows, :].astype(F32)
        d_base = d_tokens[rows, :].astype(F32)
        d_base = jnp.where(live, d_base, jnp.zeros_like(d_base))
        result[rows, :] = (base + scale * primal).astype(BF)
        d_result[rows, :] = (d_base + scale * tangent).astype(BF)


def per_device(
    queries,
    d_queries,
    key_rows,
    value_rows,
    d_key_rows,
    d_value_rows,
    live_flags,
    out_weight,
    gate_scale,
    tokens,
    d_tokens,
):
    rows, width = queries.shape
    columns = tokens.shape[1]
    t, m = lax.axis_index(TM), lax.axis_index(MP)
    odd = (t // NY % 2).astype(jnp.int32).reshape(1)
    core = (m % 2).astype(jnp.int32).reshape(1)
    group = 4 * columns

    def shape(*dims):
        return jax.ShapeDtypeStruct(dims, BF)

    def after(a, b):
        return lax.optimization_barrier((a, b))[0]

    def exchange(a, axes):
        return lax.all_to_all(a, axes, 0, 0, tiled=True)

    def y(a, k):
        return lax.ppermute(a, TM, over_y(k))

    def z(a, k):
        return lax.ppermute(a, TM, over_z(k))

    qd, kv, other_head = pl.pallas_call(
        pack_kernel,
        out_shape=[shape(2 * rows, 2 * HD), shape(2 * rows, 4 * HD), shape(rows, 6 * HD)],
        in_specs=[SMEM_SPEC] * 2 + [HBM_SPEC] * 6,
        out_specs=[HBM_SPEC] * 3,
        scratch_shapes=[pltpu.VMEM((rows, width), BF)] * 6
        + [
            pltpu.VMEM((rows, 2 * HD), BF),
            pltpu.VMEM((rows, 4 * HD), BF),
            pltpu.VMEM((rows, 6 * HD), BF),
            pltpu.SemaphoreType.DMA((6,)),
        ],
        compiler_params=params(60),
        name="pack",
    )(odd, live_flags, queries, d_queries, key_rows, value_rows, d_key_rows, d_value_rows)
    weights = pl.pallas_call(
        cut_kernel,
        out_shape=shape(NX, width, group),
        in_specs=[HBM_SPEC],
        out_specs=HBM_SPEC,
        scratch_shapes=[pltpu.VMEM(out_weight.shape, BF), pltpu.SemaphoreType.DMA((NX,))],
        compiler_params=params(60),
        name="cut",
    )(after(out_weight, kv))
    got = z(other_head, 1)
    got = after(got, weights)
    qd, kv = pl.pallas_call(
        join_kernel,
        out_shape=[shape(2 * rows, 2 * HD), shape(2 * rows, 4 * HD)],
        in_specs=[HBM_SPEC] * 3,
        out_specs=[HBM_SPEC] * 2,
        scratch_shapes=[pltpu.VMEM((rows, 6 * HD), BF), pltpu.SemaphoreType.DMA((2,))],
        input_output_aliases={1: 0, 2: 1},
        compiler_params=params(60),
        name="join",
    )(got, qd, kv)
    kv_far = z(kv, 2)
    near_rows = [y(kv, k) for k in (1, 3, 2)]
    qd_far = z(after(qd, (near_rows[:2], kv_far)), 4)
    kv = [kv] + near_rows + [kv_far] + [y(kv_far, k) for k in (1, 3, 2)]

    w_own = exchange(after(weights, got), "x")
    qd_far = after(qd_far, w_own)

    def attend(piece):
        part = shape(2 * (rows + STAT_ROWS), 2 * HD)
        return pl.pallas_call(
            attend_kernel,
            out_shape=part,
            in_specs=[HBM_SPEC] * 9,
            out_specs=HBM_SPEC,
            scratch_shapes=[
                pltpu.VMEM((16 * rows, 4 * HD), BF),
                pltpu.VMEM((2 * rows, 2 * HD), BF),
                pltpu.VMEM(part.shape, BF),
                pltpu.SemaphoreType.DMA((9,)),
            ],
            compiler_params=params(60),
            name="attend",
        )(*kv, piece)

    far = attend(qd_far)
    near = attend(after(qd, far))
    returned = z(far, 4)

    w_other = lax.ppermute(after(w_own, far), MP, flip(1))

    acts = pl.pallas_call(
        merge_kernel,
        out_shape=shape(4 * NX, rows, HD),
        in_specs=[SMEM_SPEC] + [VMEM_SPEC] * 2,
        out_specs=HBM_SPEC,
        scratch_shapes=[pltpu.VMEM((2, 2, rows, HD), BF), pltpu.SemaphoreType.DMA((2 * NX,))],
        compiler_params=params(60),
        name="merge",
    )(odd, near, returned)
    acts = exchange(acts, ("z0", "x", "core"))

    half = (m // 2 % 2).astype(jnp.int32).reshape(1)

    def project(which, dtype):
        return pl.pallas_call(
            project_kernel,
            out_shape=[jax.ShapeDtypeStruct((rows, columns), dtype), shape(rows, columns)],
            in_specs=[SMEM_SPEC] + [VMEM_SPEC] * 3,
            out_specs=[VMEM_SPEC] * 2,
            compiler_params=params(24),
            name="project",
        )(jnp.concatenate([which, core]), acts, w_own, w_other)

    z_send, both_send = project(1 - half, BF)
    mine, core_send = project(half, F32)
    z_got = lax.ppermute(z_send, MP, flip(2))
    both_got = lax.ppermute(both_send, MP, flip(3))
    core_got = lax.ppermute(core_send, MP, flip(1))

    result, d_result = pl.pallas_call(
        finish_kernel,
        out_shape=[shape(rows, columns)] * 2,
        in_specs=[SMEM_SPEC] * 2 + [VMEM_SPEC] * 7,
        out_specs=[VMEM_SPEC] * 2,
        compiler_params=params(8),
        name="finish",
    )(
        core,
        live_flags,
        mine,
        z_got,
        core_got,
        both_got,
        gate_scale.reshape(1, columns),
        tokens,
        d_tokens,
    )
    return (result, d_result)


def solution(mesh):
    parts = mesh.devices.reshape(NZ // 2, 2, NY, NX, 2, 2)
    placed = (
        P(TM, MP),
        P(TM, MP),
        P(TM, MP),
        P(TM, MP),
        P(TM, MP),
        P(TM, MP),
        P(TM),
        P(MP, None),
        P(MP),
        P(TM, MP),
        P(TM, MP),
    )
    return jax.shard_map(
        per_device,
        mesh=Mesh(parts, TM + MP),
        in_specs=placed,
        out_specs=(P(TM, MP), P(TM, MP)),
        check_vma=False,
    )
```

```python
import functools
import math

import jax
import jax.numpy as jnp
from jax import lax
from jax.experimental import pallas as pl
from jax.experimental.pallas import tpu as pltpu
from jax.sharding import Mesh
from jax.sharding import PartitionSpec as P

HD = 128
FRAME = 32
NZ, NY, NX = 8, 4, 4
TM, MP = ("z", "z0", "y"), ("x", "half", "core")
FACTOR = 1.0 / math.sqrt(HD)
LOG2E = math.log2(math.e)
STAT_ROWS = 16
BF = jnp.bfloat16
F32 = jnp.float32
def params(mib):
    return pltpu.CompilerParams(vmem_limit_bytes=mib * 1024 * 1024)


SMEM_SPEC = pl.BlockSpec(memory_space=pltpu.SMEM)
VMEM_SPEC = pl.BlockSpec(memory_space=pltpu.VMEM)
HBM_SPEC = pl.BlockSpec(memory_space=pltpu.HBM)


def over_z(k):
    return [(z * NY + y, (z ^ k) * NY + y) for z in range(NZ) for y in range(NY)]


def over_y(k):
    return [(z * NY + y, z * NY + (y + k) % NY) for z in range(NZ) for y in range(NY)]


def flip(bits):
    return [(i, i ^ bits) for i in range(4 * NX)]


def load(sources, held, sems):
    copies = [pltpu.make_async_copy(a, b, sems.at[i]) for i, (a, b) in enumerate(zip(sources, held))]
    for copy in copies:
        copy.start()
    for copy in copies:
        copy.wait()


def run_all(copies):
    for copy in copies:
        copy.start()
    for copy in copies:
        copy.wait()


def masked_rows(flags, f, ref):
    block = ref[pl.ds(f * FRAME, FRAME), :]
    return jnp.where(flags[f * FRAME] > 0, block, jnp.zeros_like(block))


def pack_kernel(odd, flags, *refs):
    sources, (qd_own, kv_own, other_head), held = refs[:6], refs[6:9], refs[9:15]
    qd, kv, other, sems = refs[15:]
    load(sources, held, sems)
    q, dq, k, v, dk, dv = held
    is_odd = odd[0] > 0
    rows_all = other.shape[0]
    for f in range(rows_all // FRAME):
        rows = pl.ds(f * FRAME, FRAME)
        blocks = (
            masked_rows(flags, f, dq),
            q[rows, :],
            k[rows, :],
            masked_rows(flags, f, dk),
            v[rows, :],
            masked_rows(flags, f, dv),
        )
        for i, block in enumerate(blocks):
            first, second = block[:, :HD], block[:, HD:]
            own = jnp.where(is_odd, second, first)
            other[rows, i * HD : (i + 1) * HD] = jnp.where(is_odd, first, second)
            if i < 2:
                qd[rows, i * HD : (i + 1) * HD] = own
            else:
                kv[rows, (i - 2) * HD : (i - 1) * HD] = own
    top = pl.ds(0, rows_all)
    run_all(
        [
            pltpu.make_async_copy(other, other_head, sems.at[0]),
            pltpu.make_async_copy(qd, qd_own.at[top], sems.at[1]),
            pltpu.make_async_copy(kv, kv_own.at[top], sems.at[2]),
        ]
    )


def join_kernel(got, qd_in, kv_in, qd, kv, held, sems):
    del qd_in, kv_in
    rows = got.shape[0]
    below = pl.ds(rows, rows)
    run_all([pltpu.make_async_copy(got, held, sems.at[0])])
    run_all(
        [
            pltpu.make_async_copy(held.at[:, pl.ds(0, 2 * HD)], qd.at[below], sems.at[0]),
            pltpu.make_async_copy(held.at[:, pl.ds(2 * HD, 4 * HD)], kv.at[below], sems.at[1]),
        ]
    )


def cut_kernel(w_in, w_out, held, sems):
    group = w_out.shape[2]
    run_all([pltpu.make_async_copy(w_in, held, sems.at[0])])
    run_all(
        [
            pltpu.make_async_copy(held.at[:, pl.ds(i * group, group)], w_out.at[i], sems.at[i])
            for i in range(NX)
        ]
    )


def in_three(value):
    high = value.astype(BF).astype(F32)
    middle = (value - high).astype(BF).astype(F32)
    low = (value - high - middle).astype(BF).astype(F32)
    return high, middle, low


def attend_kernel(*refs):
    kv_in, qd_in, out = refs[:8], refs[8], refs[9]
    kv, qd, held, sems = refs[10:]
    rows = kv_in[0].shape[0]
    half = rows // 2
    copies = [pltpu.make_async_copy(qd_in, qd, sems.at[8])]
    for i in range(8):
        copies.append(pltpu.make_async_copy(kv_in[i], kv.at[pl.ds(i * rows, rows)], sems.at[i]))
    for copy in copies:
        copy.start()
    contract = (((1,), (1,)), ((), ()))
    copies[0].wait()
    both = qd[...]
    parts = (slice(0, 4 * rows), slice(4 * rows, 8 * rows))
    scores, slopes = [], []
    for p, at in enumerate(parts):
        for copy in copies[1 + 4 * p : 5 + 4 * p]:
            copy.wait()
        scores.append(
            lax.dot_general(both[:, HD:], kv[at, :HD], contract, preferred_element_type=F32)
        )
        slopes.append(
            lax.dot_general(both, kv[at, : 2 * HD], contract, preferred_element_type=F32)
        )
    peak = jnp.maximum(*[jnp.max(part, axis=1, keepdims=True) for part in scores])
    peak = peak * (FACTOR * LOG2E)
    total, slope, weighted, tangent = 0.0, 0.0, 0.0, 0.0
    for at, score, d_score in zip(parts, scores, slopes):
        weights = jnp.exp2(score * (FACTOR * LOG2E) - peak)
        product = weights * d_score
        total += jnp.sum(weights, axis=1, keepdims=True)
        slope += jnp.sum(product, axis=1, keepdims=True)
        weighted += jnp.dot(weights.astype(BF), kv[at, 2 * HD :], preferred_element_type=F32)
        tangent += jnp.dot(
            product.astype(BF), kv[at, 2 * HD : 3 * HD], preferred_element_type=F32
        )
    inverse = 1.0 / total
    mean = slope * (inverse * FACTOR)
    primal = weighted[:, :HD] * inverse
    tangent = (tangent * FACTOR + weighted[:, HD:]) * inverse - mean * primal
    lanes = lax.broadcasted_iota(jnp.int32, (rows, HD), 1)
    stats = jnp.zeros((rows, HD), F32)
    for i, part in enumerate(in_three(peak + jnp.log2(total)) + in_three(mean)):
        stats = jnp.where(lanes == i, part, stats)
    for p in range(2):
        mine = slice(p * half, (p + 1) * half)
        at = p * (half + STAT_ROWS)
        held[at : at + half, :HD] = primal[mine].astype(BF)
        held[at : at + half, HD:] = tangent[mine].astype(BF)
        tile = jnp.concatenate([stats[mine], jnp.zeros((2 * HD - half, HD), F32)], axis=0)
        held[at + half : at + half + STAT_ROWS, :] = tile.T[:STAT_ROWS].astype(BF)
    run_all([pltpu.make_async_copy(held, out, sems.at[0])])


def merge_kernel(odd, one, two, out, merged, sems):
    rows = merged.shape[2]
    parts = (one, two)
    is_odd = odd[0] > 0
    found = []
    for p in range(2):
        at = p * (rows + STAT_ROWS)
        tiles = [part[at + rows : at + rows + STAT_ROWS, :].astype(F32) for part in parts]
        stats = jnp.concatenate(tiles * 4, axis=0).T[:rows]

        def value(i, first):
            lane = i * STAT_ROWS + first
            return sum(stats[:, lane + j : lane + j + 1] for j in range(3))

        sizes = [value(i, 0) for i in range(2)]
        means = [value(i, 3) for i in range(2)]
        peak = jnp.maximum(*sizes)
        sizes = [jnp.exp2(size - peak) for size in sizes]
        inverse = 1.0 / sum(sizes)
        sizes = [size * inverse for size in sizes]
        mean = sum(size * m for size, m in zip(sizes, means))
        primal = jnp.zeros((rows, HD), F32)
        tangent = jnp.zeros((rows, HD), F32)
        for part, size, m in zip(parts, sizes, means):
            a = part[at : at + rows, :HD].astype(F32)
            primal += size * a
            tangent += size * part[at : at + rows, HD:].astype(F32) + (size * (m - mean)) * a
        found.append((primal.astype(BF), tangent.astype(BF)))
    for kind in range(2):
        own, other = found[0][kind], found[1][kind]
        merged[0, kind] = jnp.where(is_odd, other, own)
        merged[1, kind] = jnp.where(is_odd, own, other)
    copies = []
    for parity in range(2):
        for i in range(NX):
            j = parity * NX + i
            copies.append(
                pltpu.make_async_copy(merged.at[parity], out.at[pl.ds(2 * j, 2)], sems.at[j])
            )
    run_all(copies)


def project_kernel(place, acts, w_own, w_other, mine, others):
    width = mine.shape[1]
    c = place[1]
    for half in range(2):

        @pl.when(place[0] == half)
        def _():
            columns = slice(2 * half * width, 2 * (half + 1) * width)
            total = jnp.zeros((mine.shape[0], 2 * width), F32)
            for k in range(NX):
                for w, i in ((w_own, 2 * k + c), (w_other, 2 * k + 1 - c)):
                    heads = jnp.concatenate([acts[i], acts[2 * NX + i]], axis=1)
                    total += jnp.dot(heads, w[k, :, columns], preferred_element_type=F32)
            first, second = total[:, :width], total[:, width:]
            mine[...] = jnp.where(c > 0, second, first).astype(mine.dtype)
            others[...] = jnp.where(c > 0, first, second).astype(others.dtype)


def finish_kernel(
    core, flags, mine, z_got, core_got, both_got, gate, tokens, d_tokens, result, d_result
):
    is_second = core[0] > 0
    scale = gate[...]
    for f in range(tokens.shape[0] // FRAME):
        rows = pl.ds(f * FRAME, FRAME)
        live = flags[f * FRAME] > 0
        kept = mine[rows, :] + z_got[rows, :].astype(F32)
        other = core_got[rows, :].astype(F32) + both_got[rows, :].astype(F32)
        primal = jnp.where(is_second, other, kept)
        tangent = jnp.where(is_second, kept, other)
        base = tokens[rows, :].astype(F32)
        d_base = d_tokens[rows, :].astype(F32)
        d_base = jnp.where(live, d_base, jnp.zeros_like(d_base))
        result[rows, :] = (base + scale * primal).astype(BF)
        d_result[rows, :] = (d_base + scale * tangent).astype(BF)


def per_device(
    queries,
    d_queries,
    key_rows,
    value_rows,
    d_key_rows,
    d_value_rows,
    live_flags,
    out_weight,
    gate_scale,
    tokens,
    d_tokens,
):
    rows, width = queries.shape
    columns = tokens.shape[1]
    t, m = lax.axis_index(TM), lax.axis_index(MP)
    odd = (t // NY % 2).astype(jnp.int32).reshape(1)
    core = (m % 2).astype(jnp.int32).reshape(1)
    group = 4 * columns

    def shape(*dims):
        return jax.ShapeDtypeStruct(dims, BF)

    def after(a, b):
        return lax.optimization_barrier((a, b))[0]

    def exchange(a, axes):
        return lax.all_to_all(a, axes, 0, 0, tiled=True)

    def y(a, k):
        return lax.ppermute(a, TM, over_y(k))

    def z(a, k):
        return lax.ppermute(a, TM, over_z(k))

    qd, kv, other_head = pl.pallas_call(
        pack_kernel,
        out_shape=[shape(2 * rows, 2 * HD), shape(2 * rows, 4 * HD), shape(rows, 6 * HD)],
        in_specs=[SMEM_SPEC] * 2 + [HBM_SPEC] * 6,
        out_specs=[HBM_SPEC] * 3,
        scratch_shapes=[pltpu.VMEM((rows, width), BF)] * 6
        + [
            pltpu.VMEM((rows, 2 * HD), BF),
            pltpu.VMEM((rows, 4 * HD), BF),
            pltpu.VMEM((rows, 6 * HD), BF),
            pltpu.SemaphoreType.DMA((6,)),
        ],
        compiler_params=params(60),
        name="pack",
    )(odd, live_flags, queries, d_queries, key_rows, value_rows, d_key_rows, d_value_rows)
    weights = pl.pallas_call(
        cut_kernel,
        out_shape=shape(NX, width, group),
        in_specs=[HBM_SPEC],
        out_specs=HBM_SPEC,
        scratch_shapes=[pltpu.VMEM(out_weight.shape, BF), pltpu.SemaphoreType.DMA((NX,))],
        compiler_params=params(60),
        name="cut",
    )(after(out_weight, kv))
    got = z(other_head, 1)
    got = after(got, weights)
    qd, kv = pl.pallas_call(
        join_kernel,
        out_shape=[shape(2 * rows, 2 * HD), shape(2 * rows, 4 * HD)],
        in_specs=[HBM_SPEC] * 3,
        out_specs=[HBM_SPEC] * 2,
        scratch_shapes=[pltpu.VMEM((rows, 6 * HD), BF), pltpu.SemaphoreType.DMA((2,))],
        input_output_aliases={1: 0, 2: 1},
        compiler_params=params(60),
        name="join",
    )(got, qd, kv)
    kv_far = z(kv, 2)
    near_rows = [y(kv, k) for k in (1, 3, 2)]
    qd_far = z(after(qd, (near_rows[:2], kv_far)), 4)
    kv = [kv] + near_rows + [kv_far] + [y(kv_far, k) for k in (1, 3, 2)]

    w_own = exchange(after(weights, got), "x")
    qd_far = after(qd_far, w_own)

    def attend(piece):
        part = shape(2 * (rows + STAT_ROWS), 2 * HD)
        return pl.pallas_call(
            attend_kernel,
            out_shape=part,
            in_specs=[HBM_SPEC] * 9,
            out_specs=HBM_SPEC,
            scratch_shapes=[
                pltpu.VMEM((16 * rows, 4 * HD), BF),
                pltpu.VMEM((2 * rows, 2 * HD), BF),
                pltpu.VMEM(part.shape, BF),
                pltpu.SemaphoreType.DMA((9,)),
            ],
            compiler_params=params(60),
            name="attend",
        )(*kv, piece)

    far = attend(qd_far)
    near = attend(after(qd, far))
    returned = z(far, 4)

    w_other = lax.ppermute(after(w_own, far), MP, flip(1))

    acts = pl.pallas_call(
        merge_kernel,
        out_shape=shape(4 * NX, rows, HD),
        in_specs=[SMEM_SPEC] + [VMEM_SPEC] * 2,
        out_specs=HBM_SPEC,
        scratch_shapes=[pltpu.VMEM((2, 2, rows, HD), BF), pltpu.SemaphoreType.DMA((2 * NX,))],
        compiler_params=params(60),
        name="merge",
    )(odd, near, returned)
    acts = exchange(acts, ("z0", "x", "core"))

    half = (m // 2 % 2).astype(jnp.int32).reshape(1)

    def project(which, dtype):
        return pl.pallas_call(
            project_kernel,
            out_shape=[jax.ShapeDtypeStruct((rows, columns), dtype), shape(rows, columns)],
            in_specs=[SMEM_SPEC] + [VMEM_SPEC] * 3,
            out_specs=[VMEM_SPEC] * 2,
            compiler_params=params(24),
            name="project",
        )(jnp.concatenate([which, core]), acts, w_own, w_other)

    z_send, both_send = project(1 - half, BF)
    mine, core_send = project(half, F32)
    z_got = lax.ppermute(z_send, MP, flip(2))
    both_got = lax.ppermute(both_send, MP, flip(3))
    core_got = lax.ppermute(core_send, MP, flip(1))

    result, d_result = pl.pallas_call(
        finish_kernel,
        out_shape=[shape(rows, columns)] * 2,
        in_specs=[SMEM_SPEC] * 2 + [VMEM_SPEC] * 7,
        out_specs=[VMEM_SPEC] * 2,
        compiler_params=params(8),
        name="finish",
    )(
        core,
        live_flags,
        mine,
        z_got,
        core_got,
        both_got,
        gate_scale.reshape(1, columns),
        tokens,
        d_tokens,
    )
    return (result, d_result)


def solution(mesh):
    parts = mesh.devices.reshape(NZ // 2, 2, NY, NX, 2, 2)
    placed = (
        P(TM, MP),
        P(TM, MP),
        P(TM, MP),
        P(TM, MP),
        P(TM, MP),
        P(TM, MP),
        P(TM),
        P(MP, None),
        P(MP),
        P(TM, MP),
        P(TM, MP),
    )
    return jax.shard_map(
        per_device,
        mesh=Mesh(parts, TM + MP),
        in_specs=placed,
        out_specs=(P(TM, MP), P(TM, MP)),
        check_vma=False,
    )
```
